768 devices in a mesh: dp: 48 (over x, z), tensor: 16 (over y, core).
Axes of the slice: x: 4, y: 8, z: 12, core: 2. Of those that a mesh axis runs over, the one named last changes fastest.
Arguments:
- lengths: int32 [144], replicated, may hold values from 0 to 1536, as said below
- queries: bfloat16 [18432, 8192], P('dp', 'tensor'), may hold values from -6 to 6
- keys: bfloat16 [18432, 1024], P('dp'), may hold values from -6 to 6
- values: bfloat16 [18432, 1024], P('dp'), may hold values from -6 to 6
- out_weight: bfloat16 [8192, 8192], P('tensor'), may hold values from -0.29882812 to 0.29882812
Outputs:
- projected: bfloat16 [18432, 8192], P('dp', 'tensor')
The draws below stay inside these ranges and needn't reach their ends.
Inputs may be any that keep to these rules, and one draw needn't show every extreme that they name: `lengths`: entries are multiples of 128; the positive ones come first and sum to 18432, zeros follow; one entry equals 1536.
All inputs are finite; a program needn't handle non-finite values.
Results may differ from the reference program's by a relative error of at most 0.023.
Values may be sent and summed in bfloat16 or wider, within the bound.
No kernel may reach another device: no remote copies, remote signals or barrier semaphores. Data moves between devices by JAX's collectives and lax.ppermute only.
A program may use at most 64 MiB of HBM per device.

```python
import jax
import jax.numpy as jnp
from jax import lax

D = 8192
HQ = 64
KVH = 8
HD = 128
TOK_DEV = 384
UNIT = 128
SPAN = 4
DOCMAX = 1536
TOKENS = 18432
N_DP = 48
N_TENSOR = 16


def draw_queries(key, part):
    key = jax.random.fold_in(key, 1)
    result = jnp.clip(jax.random.normal(key, (TOKENS, HQ * HD), jnp.float32), -6.0, 6.0)
    return result.astype(jnp.bfloat16)


def draw_keys(key, part):
    key = jax.random.fold_in(key, 2)
    result = jnp.clip(jax.random.normal(key, (TOKENS, KVH * HD), jnp.float32), -6.0, 6.0)
    return result.astype(jnp.bfloat16)


def draw_lengths(key, part):
    key = jax.random.fold_in(key, 3)
    cells = TOKENS // UNIT
    longest = DOCMAX // UNIT
    units = jax.random.randint(jax.random.fold_in(key, 1), (cells,), 1, longest + 1)
    forced = jax.random.randint(jax.random.fold_in(key, 2), (), 0, 2)
    units = jnp.where(jnp.arange(cells, dtype=jnp.int32) == forced, longest, units)
    ends = jnp.cumsum(units)
    starts = ends - units
    kept = jnp.where(ends <= cells, units, jnp.where(starts < cells, cells - starts, 0))
    return (kept * UNIT).astype(jnp.int32)


def spiked(entries, key, source, target, shards_of, factor):
    owner, partner = [(jnp.arange(entries.shape[axis_at]) // (entries.shape[axis_at] // shards_of)).reshape([-1 if axis == axis_at else 1 for axis in range(entries.ndim)]) for axis_at in (source, target)]
    chosen = jax.random.permutation(key, shards_of)[partner]
    strong = (owner == chosen) | (owner == (partner + shards_of // 2) % shards_of)
    return jnp.where(strong, factor * entries, entries)


def steps_of(own_key, dims, cuts, least, top_value):
    gain, own = 1.0, jax.random.fold_in(own_key, 6)
    for position, blocks in cuts:
        steps = jnp.exp(jax.random.uniform(jax.random.fold_in(own, position), (blocks,), jnp.float32, least / len(cuts), top_value / len(cuts)))
        gain = gain * jnp.repeat(steps, dims[position] // blocks).reshape([-1 if axis == position else 1 for axis in range(len(dims))])
    return gain


def centred(key, extent, spread, reach, pieces=(), held_as=jnp.bfloat16):
    values = jax.random.normal(key, extent, jnp.float32) * spread
    if len(pieces) > 0:
        values = steps_of(key, extent, pieces, -0.22, 0.18) * values
    return jnp.clip(values, min=-reach, max=reach).astype(held_as)


def gaussian_with(stream_key, dims, deviation, most, cuts, heavy, kind=jnp.bfloat16):
    values = deviation * jax.random.normal(stream_key, dims, jnp.float32)
    if cuts:
        values = values * steps_of(stream_key, dims, cuts, -0.22, 0.18)
    return jnp.clip(spiked(values, jax.random.fold_in(stream_key, 3), *heavy), -most, most).astype(kind)


def setup_inputs(seed: int = 0) -> dict:
    key_list = jax.random.split(jax.random.key(seed), 6)
    return {
        "lengths": draw_lengths(jax.random.fold_in(key_list[5], 71), 0),
        "queries": draw_queries(jax.random.fold_in(key_list[5], 71), 0),
        "keys": draw_keys(jax.random.fold_in(key_list[5], 71), 0),
        "values": centred(key_list[3], (TOKENS, KVH * HD), 1.0, 6.0, ((0, 48),)),
        "out_weight": gaussian_with(key_list[4], (HQ * HD, D), 0.05, 0.29882812, ((0, 16),), (0, 1, 16, 2.0)),
    }


def doc_index(positions, lengths):
    ends = jnp.cumsum(lengths)
    return jnp.sum((ends[None, :] <= positions[:, None]).astype(jnp.int32), axis=1)


def reference(lengths, queries, keys, values, out_weight):
    group = HQ // KVH
    window = (SPAN + 1) * TOK_DEV
    front = jnp.zeros((SPAN * TOK_DEV, KVH * HD), keys.dtype)
    key_pad = jnp.concatenate([front, keys], axis=0)
    val_pad = jnp.concatenate([front, values], axis=0)
    scale = 1.0 / (HD ** 0.5)

    def one_block(block):
        q_start = (block * TOK_DEV).astype(jnp.int32)
        q_rows = lax.dynamic_slice_in_dim(queries, q_start, TOK_DEV, 0)
        q_rows = q_rows.astype(jnp.float32).reshape(TOK_DEV, HQ, HD)
        k_rows = lax.dynamic_slice_in_dim(key_pad, q_start, window, 0).astype(jnp.float32)
        v_rows = lax.dynamic_slice_in_dim(val_pad, q_start, window, 0).astype(jnp.float32)
        k_rows = jnp.repeat(k_rows.reshape(window, KVH, HD), group, axis=1)
        v_rows = jnp.repeat(v_rows.reshape(window, KVH, HD), group, axis=1)
        q_pos = q_start + jnp.arange(TOK_DEV, dtype=jnp.int32)
        k_pos = q_start - SPAN * TOK_DEV + jnp.arange(window, dtype=jnp.int32)
        q_doc = doc_index(q_pos, lengths)
        k_doc = doc_index(jnp.maximum(k_pos, 0), lengths)
        allowed = (k_pos[None, :] <= q_pos[:, None]) & (k_pos[None, :] >= 0) & (k_doc[None, :] == q_doc[:, None])
        scores = jnp.einsum('qhd,khd->hqk', q_rows, k_rows) * scale
        masked = jnp.where(allowed[None], scores, -1e30)
        top = jnp.max(masked, axis=-1, keepdims=True)
        weights = jnp.where(allowed[None], jnp.exp(scores - top), 0.0)
        total = jnp.sum(weights, axis=-1)
        rounded = weights.astype(jnp.bfloat16).astype(jnp.float32)
        attended = jnp.einsum('hqk,khd->qhd', rounded, v_rows) / jnp.transpose(total)[:, :, None]
        return attended.astype(jnp.bfloat16).reshape(TOK_DEV, HQ * HD)

    attended = lax.map(one_block, jnp.arange(N_DP, dtype=jnp.int32)).reshape(TOKENS, HQ * HD)
    rows_each = (HQ * HD) // N_TENSOR

    def add_part(index, summed):
        start = (index * rows_each).astype(jnp.int32)
        left = lax.dynamic_slice_in_dim(attended, start, rows_each, 1)
        right = lax.dynamic_slice_in_dim(out_weight, start, rows_each, 0)
        part = jnp.dot(left, right, preferred_element_type=jnp.float32).astype(jnp.bfloat16)
        part = lax.optimization_barrier(part)
        return summed + part.astype(jnp.float32)

    summed = lax.fori_loop(0, N_TENSOR, add_part, jnp.zeros((TOKENS, D), jnp.float32))
    return summed.astype(jnp.bfloat16)
```

```python
import functools
import math

import jax
import jax.numpy as jnp
from jax import lax
from jax.experimental import pallas as pl
from jax.experimental.pallas import tpu as pltpu
from jax.sharding import Mesh, PartitionSpec as P

HD = 128
UNIT = 128
NEG = -1e30
EXP_SCALE = math.log2(math.e) / HD**0.5
ROW_PARTS = 1

FIRST_BACK = (1, 3)
SECOND_BACK = (2, 4)


def block_bias(allowed):
    return jnp.where(allowed, 0.0, NEG).astype(jnp.float32)


def head_pair(q_refs, pair, unit):
    q_ref = q_refs[pair // 2]
    rows = pl.ds(unit * UNIT, UNIT)
    first = (pair % 2) * 2 * HD
    return jnp.concatenate([q_ref[rows, first : first + HD], q_ref[rows, first + HD : first + 2 * HD]], axis=0)


def raw_scores(k_rows, q_pair):
    return lax.dot_general(k_rows, q_pair, (((1,), (1,)), ((), ())), preferred_element_type=jnp.float32)


def weighted(v_rows, weights):
    return lax.dot_general(
        v_rows, weights.astype(jnp.bfloat16), (((0,), (0,)), ((), ())), preferred_element_type=jnp.float32
    )


def store_state(out_ref, pair, unit, top, total, accum):
    heads = 8
    cols = pl.ds(unit * UNIT, UNIT)
    for side in range(2):
        head = 2 * pair + side
        part = slice(side * UNIT, (side + 1) * UNIT)
        out_ref[pl.ds(head * HD, HD), cols] = accum[:, part]
        out_ref[pl.ds(heads * HD + head, 1), cols] = top[:, part]
        out_ref[pl.ds(heads * HD + heads + head, 1), cols] = total[:, part]


def load_state(ref, pair, unit):
    heads = 8
    cols = pl.ds(unit * UNIT, UNIT)
    both = []
    for base, size in ((heads * HD, 1), (heads * HD + heads, 1), (0, HD)):
        halves = [ref[pl.ds(base + (2 * pair + side) * size, size), cols] for side in range(2)]
        both.append(jnp.concatenate(halves, axis=1))
    return both


def piece_bias(info_ref, unit, back, units):
    low = info_ref[unit]
    return [block_bias(low <= block - units * back) for block in range(units)]


def attend_first(info_ref, qm_ref, qo_ref, own_ref, piece_ref, out_ref):
    units = qm_ref.shape[0] // UNIT
    core = info_ref[units + 2]
    triangle = lax.broadcasted_iota(jnp.int32, (UNIT, 2 * UNIT), 0) <= (
        lax.broadcasted_iota(jnp.int32, (UNIT, 2 * UNIT), 1) % UNIT
    )
    for unit in range(units):
        bias = piece_bias(info_ref, unit, info_ref[units], units)
        low = info_ref[unit]
        own_bias = [block_bias((low <= block) & (core == 0)) for block in range(unit + 1)]
        for pair in range(4):
            q_pair = head_pair((qm_ref, qo_ref), pair, unit)
            s = raw_scores(piece_ref[:, :HD], q_pair)
            blocks = [s[b * UNIT : (b + 1) * UNIT] + bias[b] for b in range(units)]
            span = (unit + 1) * UNIT
            s = raw_scores(own_ref[:span, :HD], q_pair)
            for b in range(unit + 1):
                block = s[b * UNIT : (b + 1) * UNIT] + own_bias[b]
                blocks.append(jnp.where(triangle, block, NEG) if b == unit else block)
            scores = jnp.concatenate(blocks, axis=0)
            top = jnp.max(scores, axis=0, keepdims=True)
            weights = jnp.exp2((scores - top) * EXP_SCALE)
            total = jnp.sum(weights, axis=0, keepdims=True)
            rows = units * UNIT
            accum = weighted(piece_ref[:, HD:], weights[:rows]) + weighted(own_ref[:span, HD:], weights[rows:])
            store_state(out_ref, pair, unit, top, total, accum)


def attend_second(info_ref, qm_ref, qo_ref, piece_ref, state_ref, out_ref):
    units = qm_ref.shape[0] // UNIT
    for unit in range(units):
        bias = piece_bias(info_ref, unit, info_ref[units + 1], units)
        for pair in range(4):
            q_pair = head_pair((qm_ref, qo_ref), pair, unit)
            s = raw_scores(piece_ref[:, :HD], q_pair)
            scores = jnp.concatenate([s[b * UNIT : (b + 1) * UNIT] + bias[b] for b in range(units)], axis=0)
            old_top, old_total, old_accum = load_state(state_ref, pair, unit)
            top = jnp.maximum(old_top, jnp.max(scores, axis=0, keepdims=True))
            weights = jnp.exp2((scores - top) * EXP_SCALE)
            factor = jnp.exp2((old_top - top) * EXP_SCALE)
            total = old_total * factor + jnp.sum(weights, axis=0, keepdims=True)
            accum = old_accum * factor + weighted(piece_ref[:, HD:], weights)
            store_state(out_ref, pair, unit, top, total, accum)


def combine(here_ref, there_ref, out_ref):
    heads = 8
    for head in range(heads):
        other = (head + heads // 2) % heads
        top_a = here_ref[pl.ds(heads * HD + head, 1), :]
        top_b = there_ref[pl.ds(heads * HD + other, 1), :]
        top = jnp.maximum(top_a, top_b)
        share_a = jnp.exp2((top_a - top) * EXP_SCALE)
        share_b = jnp.exp2((top_b - top) * EXP_SCALE)
        total = (
            here_ref[pl.ds(heads * HD + heads + head, 1), :] * share_a
            + there_ref[pl.ds(heads * HD + heads + other, 1), :] * share_b
        )
        accum = here_ref[pl.ds(head * HD, HD), :] * share_a + there_ref[pl.ds(other * HD, HD), :] * share_b
        out_ref[:, head * HD : (head + 1) * HD] = jnp.transpose(accum / total).astype(jnp.bfloat16)


def project(columns_ref, att_ref, wm_ref, wo_ref, out_ref):
    del columns_ref
    depth = wm_ref.shape[0]
    summed = jnp.dot(att_ref[:, :depth], wm_ref[...], preferred_element_type=jnp.float32)
    summed += jnp.dot(att_ref[:, depth:], wo_ref[...], preferred_element_type=jnp.float32)
    out_ref[0] = summed.astype(jnp.bfloat16)


VM = pl.BlockSpec(memory_space=pltpu.VMEM)
SM = pl.BlockSpec(memory_space=pltpu.SMEM)
LIMIT = pltpu.CompilerParams(vmem_limit_bytes=32 * 1024 * 1024)


def on_device(lengths, queries, keys, values, out_weight):
    rows, wide = queries.shape
    units = rows // UNIT
    dp_count, y_count = lax.axis_size("dp"), lax.axis_size("y")
    dp, y, core = lax.axis_index("dp"), lax.axis_index("y"), lax.axis_index("core")
    swap = [(0, 1), (1, 0)]

    own = jnp.concatenate(
        [lax.dynamic_slice_in_dim(keys, y * HD, HD, 1), lax.dynamic_slice_in_dim(values, y * HD, HD, 1)], axis=1
    )
    first_pairs = [
        (2 * i + c, 2 * (i + FIRST_BACK[c]) + c) for c in range(2) for i in range(dp_count - FIRST_BACK[c])
    ]
    first = lax.ppermute(own, ("dp", "core"), first_pairs)
    q_other = lax.ppermute(queries, "core", swap)
    w_other = lax.ppermute(out_weight, "core", swap)
    second = lax.ppermute(first, "dp", [(i, i + 1) for i in range(dp_count - 1)])

    order = jnp.arange(lengths.shape[0], dtype=jnp.int32)
    ends = jnp.sum(jnp.where(order[None, :] <= order[:, None], lengths[None, :], 0), axis=1)
    q_starts = dp * rows + UNIT * jnp.arange(units, dtype=jnp.int32)
    doc_starts = jnp.max(jnp.where(ends[None, :] <= q_starts[:, None], ends[None, :], 0), axis=1)
    lows = doc_starts // UNIT - dp * units
    tail = jnp.stack([1 + 2 * core, 2 + 2 * core, core])
    info = jnp.concatenate([lows, tail]).astype(jnp.int32)

    state_shape = jax.ShapeDtypeStruct((2 * wide + 16, rows), jnp.float32)
    state = pl.pallas_call(
        attend_first,
        out_shape=state_shape,
        in_specs=[SM, VM, VM, VM, VM],
        out_specs=VM,
        compiler_params=LIMIT,
        cost_estimate=pl.CostEstimate(flops=1_200_000_000, bytes_accessed=4_000_000, transcendentals=2_000_000),
    )(info, queries, q_other, own, first)
    state = pl.pallas_call(
        attend_second,
        out_shape=state_shape,
        in_specs=[SM, VM, VM, VM, VM],
        out_specs=VM,
        compiler_params=LIMIT,
        cost_estimate=pl.CostEstimate(flops=600_000_000, bytes_accessed=4_000_000, transcendentals=1_000_000),
    )(info, queries, q_other, second, state)
    there = lax.ppermute(state, "core", swap)
    attended = pl.pallas_call(
        combine,
        out_shape=jax.ShapeDtypeStruct((rows, 2 * wide), jnp.bfloat16),
        in_specs=[VM, VM],
        out_specs=VM,
        compiler_params=LIMIT,
        cost_estimate=pl.CostEstimate(flops=2_000_000, bytes_accessed=4_000_000, transcendentals=10_000),
    )(state, there)

    def part(columns):
        count = columns.shape[0]
        return pl.pallas_call(
            project,
            out_shape=jax.ShapeDtypeStruct((count, rows, wide), jnp.bfloat16),
            grid_spec=pltpu.PrefetchScalarGridSpec(
                num_scalar_prefetch=1,
                grid=(count,),
                in_specs=[
                    pl.BlockSpec((rows, 2 * wide), lambda g, cols: (0, 0)),
                    pl.BlockSpec((wide, wide), lambda g, cols: (0, cols[g])),
                    pl.BlockSpec((wide, wide), lambda g, cols: (0, cols[g])),
                ],
                out_specs=pl.BlockSpec((1, rows, wide), lambda g, cols: (g, 0, 0)),
            ),
            compiler_params=LIMIT,
            cost_estimate=pl.CostEstimate(
                flops=4 * rows * wide * wide * count, bytes_accessed=3_000_000 * count, transcendentals=0
            ),
        )(columns, attended, out_weight, w_other)

    half = y_count // 2
    way = 1 - 2 * core

    def columns_at(distance):
        chunk = jnp.mod(y + way * distance, y_count)
        return jnp.stack([2 * chunk + core, 2 * chunk + 1 - core]).astype(jnp.int32)

    straight = [(2 * i + c, 2 * ((i + 1 - 2 * c) % y_count) + c) for i in range(y_count) for c in range(2)]
    cross = [(2 * i + c, 2 * ((i + 1 - 2 * c) % y_count) + 1 - c) for i in range(y_count) for c in range(2)]
    axes = ("y", "core")
    size = rows // ROW_PARTS

    def add(a, *others):
        total = a.astype(jnp.float32)
        for b in others:
            total = total + b.astype(jnp.float32)
        return total.astype(jnp.bfloat16)

    parts = {half: part(columns_at(half)[:1])}
    for distance in range(half - 1, 0, -1):
        parts[distance] = part(columns_at(distance))
    mine = part(columns_at(0)[:1])[0]
    outs = []
    for r in range(ROW_PARTS):
        at = slice(r * size, (r + 1) * size)
        got = lax.ppermute(parts[half][0, at], axes, straight)
        for distance in range(half - 1, 0, -1):
            now = parts[distance][:, at]
            if distance == half - 1:
                send = jnp.stack([add(now[0], got), now[1]])
            else:
                send = add(now, got)
            if distance > 1:
                got = lax.ppermute(send, axes, straight)
        near = lax.ppermute(send[0], axes, straight)
        far = lax.ppermute(send[1], axes, cross)
        outs.append(add(mine[at], near, far))
    return jnp.concatenate(outs, axis=0) if ROW_PARTS > 1 else outs[0]


def solution(mesh):
    dp_count, tensor_count = mesh.shape["dp"], mesh.shape["tensor"]
    split = Mesh(mesh.devices.reshape(dp_count, tensor_count // 2, 2), ("dp", "y", "core"))
    heads = ("y", "core")
    placed = (P(), P("dp", heads), P("dp", None), P("dp", None), P(heads, None))
    return jax.shard_map(on_device, mesh=split, in_specs=placed, out_specs=P("dp", heads), check_vma=False)
```

```python
import functools
import math

import jax
import jax.numpy as jnp
from jax import lax
from jax.experimental import pallas as pl
from jax.experimental.pallas import tpu as pltpu
from jax.sharding import Mesh, PartitionSpec as P

HD = 128
UNIT = 128
NEG = -1e30
EXP_SCALE = math.log2(math.e) / HD**0.5
ROW_PARTS = 2
AHEAD = 3

FIRST_BACK = (1, 3)
SECOND_BACK = (2, 4)


def block_bias(allowed):
    return jnp.where(allowed, 0.0, NEG).astype(jnp.float32)


def head_pair(q_refs, pair, unit):
    q_ref = q_refs[pair // 2]
    rows = pl.ds(unit * UNIT, UNIT)
    first = (pair % 2) * 2 * HD
    return jnp.concatenate([q_ref[rows, first : first + HD], q_ref[rows, first + HD : first + 2 * HD]], axis=0)


def raw_scores(k_rows, q_pair):
    return lax.dot_general(k_rows, q_pair, (((1,), (1,)), ((), ())), preferred_element_type=jnp.float32)


def weighted(v_columns, weights):
    return jnp.dot(v_columns, weights.astype(jnp.bfloat16), preferred_element_type=jnp.float32)


def ahead(steps, compute):
    pending = [compute(*step) for step in steps[:AHEAD]]
    for at, step in enumerate(steps):
        if at + AHEAD < len(steps):
            pending.append(compute(*steps[at + AHEAD]))
        yield step, pending.pop(0)


def store_state(out_ref, pair, unit, top, total, accum):
    heads = 8
    cols = pl.ds(unit * UNIT, UNIT)
    for side in range(2):
        head = 2 * pair + side
        part = slice(side * UNIT, (side + 1) * UNIT)
        out_ref[pl.ds(head * HD, HD), cols] = accum[:, part]
        out_ref[pl.ds(heads * HD + head, 1), cols] = top[:, part]
        out_ref[pl.ds(heads * HD + heads + head, 1), cols] = total[:, part]


def load_state(ref, pair, unit):
    heads = 8
    cols = pl.ds(unit * UNIT, UNIT)
    both = []
    for base, size in ((heads * HD, 1), (heads * HD + heads, 1), (0, HD)):
        halves = [ref[pl.ds(base + (2 * pair + side) * size, size), cols] for side in range(2)]
        both.append(jnp.concatenate(halves, axis=1))
    return both


def piece_bias(info_ref, unit, back, units):
    low = info_ref[unit]
    return [block_bias(low <= block - units * back) for block in range(units)]


def attend_own(info_ref, qm_ref, qo_ref, own_ref, out_ref):
    units = qm_ref.shape[0] // UNIT
    core = info_ref[units + 2]
    triangle = lax.broadcasted_iota(jnp.int32, (UNIT, 2 * UNIT), 0) <= (
        lax.broadcasted_iota(jnp.int32, (UNIT, 2 * UNIT), 1) % UNIT
    )
    v_own = jnp.transpose(own_ref[:, HD:])

    def scores_of(unit, pair):
        return raw_scores(own_ref[: (unit + 1) * UNIT, :HD], head_pair((qm_ref, qo_ref), pair, unit))

    steps = [(unit, pair) for unit in range(units) for pair in range(4)]
    for (unit, pair), raw in ahead(steps, scores_of):
        low = info_ref[unit]
        blocks = []
        for b in range(unit + 1):
            block = raw[b * UNIT : (b + 1) * UNIT] + block_bias((low <= b) & (core == 0))
            blocks.append(jnp.where(triangle, block, NEG) if b == unit else block)
        scores = jnp.concatenate(blocks, axis=0)
        top = jnp.max(scores, axis=0, keepdims=True)
        weights = jnp.exp2((scores - top) * EXP_SCALE)
        total = jnp.sum(weights, axis=0, keepdims=True)
        store_state(out_ref, pair, unit, top, total, weighted(v_own[:, : (unit + 1) * UNIT], weights))


def attend_piece(which, info_ref, qm_ref, qo_ref, piece_ref, state_ref, out_ref):
    units = qm_ref.shape[0] // UNIT
    v_piece = jnp.transpose(piece_ref[:, HD:])

    def scores_of(unit, pair):
        return raw_scores(piece_ref[:, :HD], head_pair((qm_ref, qo_ref), pair, unit))

    steps = [(unit, pair) for unit in range(units) for pair in range(4)]
    for (unit, pair), raw in ahead(steps, scores_of):
        bias = piece_bias(info_ref, unit, info_ref[units + which], units)
        scores = jnp.concatenate([raw[b * UNIT : (b + 1) * UNIT] + bias[b] for b in range(units)], axis=0)
        old_top, old_total, old_accum = load_state(state_ref, pair, unit)
        top = jnp.maximum(old_top, jnp.max(scores, axis=0, keepdims=True))
        weights = jnp.exp2((scores - top) * EXP_SCALE)
        factor = jnp.exp2((old_top - top) * EXP_SCALE)
        total = old_total * factor + jnp.sum(weights, axis=0, keepdims=True)
        accum = old_accum * factor + weighted(v_piece, weights)
        store_state(out_ref, pair, unit, top, total, accum)


def fetch(columns_ref, block, w_refs, w_buf, sems):
    wide = w_buf.shape[-1]
    at = pl.ds(pl.multiple_of(columns_ref[block] * wide, wide), wide)
    return [pltpu.make_async_copy(ref.at[:, at], w_buf.at[block, n], sems.at[block, n]) for n, ref in enumerate(w_refs)]


def product(att_ref, w_buf, block):
    depth = w_buf.shape[2]
    summed = jnp.dot(att_ref[:, :depth], w_buf[block, 0], preferred_element_type=jnp.float32)
    summed += jnp.dot(att_ref[:, depth:], w_buf[block, 1], preferred_element_type=jnp.float32)
    return summed.astype(jnp.bfloat16)


def combine(columns_ref, here_ref, there_ref, wm_ref, wo_ref, att_ref, out_ref, w_buf, sems):
    heads = 8
    copies = fetch(columns_ref, 0, (wm_ref, wo_ref), w_buf, sems)
    for copy in copies:
        copy.start()
    for head in range(heads):
        other = (head + heads // 2) % heads
        top_a = here_ref[pl.ds(heads * HD + head, 1), :]
        top_b = there_ref[pl.ds(heads * HD + other, 1), :]
        top = jnp.maximum(top_a, top_b)
        share_a = jnp.exp2((top_a - top) * EXP_SCALE)
        share_b = jnp.exp2((top_b - top) * EXP_SCALE)
        total = (
            here_ref[pl.ds(heads * HD + heads + head, 1), :] * share_a
            + there_ref[pl.ds(heads * HD + heads + other, 1), :] * share_b
        )
        accum = here_ref[pl.ds(head * HD, HD), :] * share_a + there_ref[pl.ds(other * HD, HD), :] * share_b
        att_ref[:, head * HD : (head + 1) * HD] = jnp.transpose(accum / total).astype(jnp.bfloat16)
    for copy in copies:
        copy.wait()
    out_ref[...] = product(att_ref, w_buf, 0)


def project(columns_ref, att_ref, wm_ref, wo_ref, out_ref, w_buf, sems):
    copies = [fetch(columns_ref, block, (wm_ref, wo_ref), w_buf, sems) for block in range(out_ref.shape[0])]
    for copy in sum(copies, []):
        copy.start()
    for block in range(out_ref.shape[0]):
        for copy in copies[block]:
            copy.wait()
        out_ref[block] = product(att_ref, w_buf, block)


VM = pl.BlockSpec(memory_space=pltpu.VMEM)
HBM = pl.BlockSpec(memory_space=pltpu.HBM)
SM = pl.BlockSpec(memory_space=pltpu.SMEM)
LIMIT = pltpu.CompilerParams(vmem_limit_bytes=32 * 1024 * 1024)
WIDE_LIMIT = pltpu.CompilerParams(vmem_limit_bytes=49 * 1024 * 1024)


def on_device(lengths, queries, keys, values, out_weight):
    rows, wide = queries.shape
    units = rows // UNIT
    dp_count, y_count = lax.axis_size("dp"), lax.axis_size("y")
    dp, y, core = lax.axis_index("dp"), lax.axis_index("y"), lax.axis_index("core")
    swap = [(0, 1), (1, 0)]

    own = jnp.concatenate(
        [lax.dynamic_slice_in_dim(keys, y * HD, HD, 1), lax.dynamic_slice_in_dim(values, y * HD, HD, 1)], axis=1
    )
    first_pairs = [
        (2 * i + c, 2 * (i + FIRST_BACK[c]) + c) for c in range(2) for i in range(dp_count - FIRST_BACK[c])
    ]
    first = lax.ppermute(own, ("dp", "core"), first_pairs)
    q_other = lax.ppermute(queries, "core", swap)
    second = lax.ppermute(first, "dp", [(i, i + 1) for i in range(dp_count - 1)])

    w_other = lax.ppermute(out_weight, "core", swap)

    order = jnp.arange(lengths.shape[0], dtype=jnp.int32)
    ends = jnp.sum(jnp.where(order[None, :] <= order[:, None], lengths[None, :], 0), axis=1)
    q_starts = dp * rows + UNIT * jnp.arange(units, dtype=jnp.int32)
    doc_starts = jnp.max(jnp.where(ends[None, :] <= q_starts[:, None], ends[None, :], 0), axis=1)
    lows = doc_starts // UNIT - dp * units
    tail = jnp.stack([1 + 2 * core, 2 + 2 * core, core])
    info = jnp.concatenate([lows, tail]).astype(jnp.int32)

    state_shape = jax.ShapeDtypeStruct((2 * wide + 16, rows), jnp.float32)
    state = pl.pallas_call(
        attend_own,
        out_shape=state_shape,
        in_specs=[SM, VM, VM, VM],
        out_specs=VM,
        compiler_params=LIMIT,
        cost_estimate=pl.CostEstimate(flops=60000000000, bytes_accessed=4_000_000, transcendentals=1_000_000),
    )(info, queries, q_other, own)
    for which, piece in enumerate((first, second)):
        state = pl.pallas_call(
            functools.partial(attend_piece, which),
            out_shape=state_shape,
            in_specs=[SM, VM, VM, VM, VM],
            out_specs=VM,
            compiler_params=LIMIT,
            cost_estimate=pl.CostEstimate(flops=60000000000, bytes_accessed=6_000_000, transcendentals=1_000_000),
        )(info, queries, q_other, piece, state)
    there = lax.ppermute(state, "core", swap)
    half = y_count // 2
    way = 1 - 2 * core

    def columns_at(distance):
        chunk = jnp.mod(y + way * distance, y_count)
        return jnp.stack([2 * chunk + core, 2 * chunk + 1 - core]).astype(jnp.int32)

    def w_scratch(count):
        return [pltpu.VMEM((count, 2, wide, wide), jnp.bfloat16), pltpu.SemaphoreType.DMA((count, 2))]

    attended, farthest = pl.pallas_call(
        combine,
        out_shape=[
            jax.ShapeDtypeStruct((rows, 2 * wide), jnp.bfloat16),
            jax.ShapeDtypeStruct((rows, wide), jnp.bfloat16),
        ],
        in_specs=[SM, VM, VM, HBM, HBM],
        out_specs=[VM, VM],
        scratch_shapes=w_scratch(1),
        compiler_params=WIDE_LIMIT,
        cost_estimate=pl.CostEstimate(flops=400_000_000, bytes_accessed=5_000_000, transcendentals=10_000),
    )(columns_at(half)[:1], state, there, out_weight, w_other)

    def part(columns):
        count = columns.shape[0]
        return pl.pallas_call(
            project,
            out_shape=jax.ShapeDtypeStruct((count, rows, wide), jnp.bfloat16),
            in_specs=[SM, VM, HBM, HBM],
            out_specs=VM,
            scratch_shapes=w_scratch(count),
            compiler_params=WIDE_LIMIT,
            cost_estimate=pl.CostEstimate(
                flops=4 * rows * wide * wide * count, bytes_accessed=3_000_000 * count, transcendentals=0
            ),
        )(columns, attended, out_weight, w_other)

    straight = [(2 * i + c, 2 * ((i + 1 - 2 * c) % y_count) + c) for i in range(y_count) for c in range(2)]
    cross = [(2 * i + c, 2 * ((i + 1 - 2 * c) % y_count) + 1 - c) for i in range(y_count) for c in range(2)]
    axes = ("y", "core")
    size = rows // ROW_PARTS

    def add(a, *others):
        total = a.astype(jnp.float32)
        for b in others:
            total = total + b.astype(jnp.float32)
        return total.astype(jnp.bfloat16)

    parts = {distance: part(columns_at(distance)) for distance in range(half - 1, 0, -1)}
    mine = part(columns_at(0)[:1])[0]
    spots = [slice(r * size, (r + 1) * size) for r in range(ROW_PARTS)]
    got = []
    for at in spots:
        value = lax.ppermute(farthest[at], axes, straight)
        got.append(lax.pad(value[None], jnp.zeros((), value.dtype), ((0, 1, 0), (0, 0, 0), (0, 0, 0))))
    token = None
    for distance in range(half - 1, 0, -1):
        for r, at in enumerate(spots):
            now = parts[distance][:, at]
            if token is not None:
                now, token = lax.optimization_barrier((now, token))
            if distance > 1:
                token = add(now, got[r])
                got[r] = lax.ppermute(token, axes, straight)
            else:
                near, far = add(now[0], got[r][0]), add(now[1], got[r][1])
                token = near
                got[r] = (lax.ppermute(near, axes, straight), lax.ppermute(far, axes, cross))
    outs = [add(mine[at], *got[r]) for r, at in enumerate(spots)]
    return jnp.concatenate(outs, axis=0) if ROW_PARTS > 1 else outs[0]


def solution(mesh):
    dp_count, tensor_count = mesh.shape["dp"], mesh.shape["tensor"]
    split = Mesh(mesh.devices.reshape(dp_count, tensor_count // 2, 2), ("dp", "y", "core"))
    heads = ("y", "core")
    placed = (P(), P("dp", heads), P("dp", None), P("dp", None), P(heads, None))
    return jax.shard_map(on_device, mesh=split, in_specs=placed, out_specs=P("dp", heads), check_vma=False)
```

```python
import functools
import math

import jax
import jax.numpy as jnp
from jax import lax
from jax.experimental import pallas as pl
from jax.experimental.pallas import tpu as pltpu
from jax.sharding import Mesh, PartitionSpec as P

HD = 128
UNIT = 128
NEG = -1e30
EXP_SCALE = math.log2(math.e) / HD**0.5
ROW_PARTS = 2
AHEAD = 3
OWN_FLOPS = 60_000_000_000
PIECE_FLOPS = (60_000_000_000, 60_000_000_000)
PROJECT_FLOPS = 60_000_000_000
STATS = 8 * HD

FIRST_BACK = (1, 3)
SECOND_BACK = (2, 4)


def block_bias(allowed):
    return jnp.where(allowed, 0.0, NEG).astype(jnp.float32)


def head_pair(q_refs, pair, unit):
    q_ref = q_refs[pair // 2]
    rows = pl.ds(unit * UNIT, UNIT)
    first = (pair % 2) * 2 * HD
    return jnp.concatenate([q_ref[rows, first : first + HD], q_ref[rows, first + HD : first + 2 * HD]], axis=0)


def raw_scores(k_rows, q_pair):
    return lax.dot_general(k_rows, q_pair, (((1,), (1,)), ((), ())), preferred_element_type=jnp.float32)


def weighted(v_columns, weights):
    return jnp.dot(v_columns, weights.astype(jnp.bfloat16), preferred_element_type=jnp.float32)


def ahead(steps, compute):
    pending = [compute(*step) for step in steps[:AHEAD]]
    for at, step in enumerate(steps):
        if at + AHEAD < len(steps):
            pending.append(compute(*steps[at + AHEAD]))
        yield step, pending.pop(0)


def store_state(out_ref, pair, unit, top, total, accum):
    heads = 8
    cols = pl.ds(unit * UNIT, UNIT)
    for side in range(2):
        head = 2 * pair + side
        part = slice(side * UNIT, (side + 1) * UNIT)
        out_ref[pl.ds(head * HD, HD), cols] = accum[:, part]
        out_ref[pl.ds(heads * HD + head, 1), cols] = top[:, part]
        out_ref[pl.ds(heads * HD + heads + head, 1), cols] = total[:, part]


def load_state(ref, pair, unit):
    heads = 8
    cols = pl.ds(unit * UNIT, UNIT)
    both = []
    for base, size in ((heads * HD, 1), (heads * HD + heads, 1), (0, HD)):
        halves = [ref[pl.ds(base + (2 * pair + side) * size, size), cols] for side in range(2)]
        both.append(jnp.concatenate(halves, axis=1))
    return both


def piece_bias(info_ref, unit, back, units):
    low = info_ref[unit]
    return [block_bias(low <= block - units * back) for block in range(units)]


def attend_own(info_ref, qm_ref, qo_ref, own_ref, out_ref):
    units = qm_ref.shape[0] // UNIT
    core = info_ref[units + 2]
    triangle = lax.broadcasted_iota(jnp.int32, (UNIT, 2 * UNIT), 0) <= (
        lax.broadcasted_iota(jnp.int32, (UNIT, 2 * UNIT), 1) % UNIT
    )
    v_own = jnp.transpose(own_ref[:, HD:])

    def scores_of(unit, pair):
        return raw_scores(own_ref[: (unit + 1) * UNIT, :HD], head_pair((qm_ref, qo_ref), pair, unit))

    steps = [(unit, pair) for unit in range(units) for pair in range(4)]
    for (unit, pair), raw in ahead(steps, scores_of):
        low = info_ref[unit]
        blocks = []
        for b in range(unit + 1):
            block = raw[b * UNIT : (b + 1) * UNIT] + block_bias((low <= b) & (core == 0))
            blocks.append(jnp.where(triangle, block, NEG) if b == unit else block)
        scores = jnp.concatenate(blocks, axis=0)
        top = jnp.max(scores, axis=0, keepdims=True)
        weights = jnp.exp2((scores - top) * EXP_SCALE)
        total = jnp.sum(weights, axis=0, keepdims=True)
        store_state(out_ref, pair, unit, top, total, weighted(v_own[:, : (unit + 1) * UNIT], weights))


def attend_piece(which, info_ref, qm_ref, qo_ref, piece_ref, state_ref, out_ref, message_ref=None):
    units = qm_ref.shape[0] // UNIT
    v_piece = jnp.transpose(piece_ref[:, HD:])

    def scores_of(unit, pair):
        return raw_scores(piece_ref[:, :HD], head_pair((qm_ref, qo_ref), pair, unit))

    steps = [(unit, pair) for unit in range(units) for pair in range(4)]
    for (unit, pair), raw in ahead(steps, scores_of):
        bias = piece_bias(info_ref, unit, info_ref[units + which], units)
        scores = jnp.concatenate([raw[b * UNIT : (b + 1) * UNIT] + bias[b] for b in range(units)], axis=0)
        old_top, old_total, old_accum = load_state(state_ref, pair, unit)
        top = jnp.maximum(old_top, jnp.max(scores, axis=0, keepdims=True))
        weights = jnp.exp2((scores - top) * EXP_SCALE)
        factor = jnp.exp2((old_top - top) * EXP_SCALE)
        total = old_total * factor + jnp.sum(weights, axis=0, keepdims=True)
        accum = old_accum * factor + weighted(v_piece, weights)
        store_state(out_ref, pair, unit, top, total, accum)
        if message_ref is not None:
            for side in range(2):
                at = pl.ds((2 * pair + side) * HD, HD), pl.ds(unit * UNIT, UNIT)
                message_ref[at] = accum[:, side * UNIT : (side + 1) * UNIT].astype(jnp.bfloat16)
    if message_ref is not None:
        rest = out_ref[STATS:, :]
        for term in range(3):
            rounded = rest.astype(jnp.bfloat16)
            message_ref[pl.ds(STATS + 16 * term, 16), :] = rounded
            rest = rest - rounded.astype(jnp.float32)


def fetch(columns_ref, block, w_refs, w_buf, sems):
    depth, wide = w_buf.shape[1] // 2, w_buf.shape[2]
    at = pl.ds(pl.multiple_of(columns_ref[block] * wide, wide), wide)
    return [
        pltpu.make_async_copy(ref.at[:, at], w_buf.at[block, pl.ds(n * depth, depth)], sems.at[block, n])
        for n, ref in enumerate(w_refs)
    ]


def product(att_ref, w_buf, block):
    return jnp.dot(att_ref[...], w_buf[block], preferred_element_type=jnp.float32).astype(jnp.bfloat16)


def combine(columns_ref, here_ref, there_ref, wm_ref, wo_ref, att_ref, out_ref, w_buf, sems):
    heads = 8
    copies = fetch(columns_ref, 0, (wm_ref, wo_ref), w_buf, sems)
    for copy in copies:
        copy.start()
    here = here_ref[STATS:, :]
    there = sum(there_ref[pl.ds(STATS + 16 * term, 16), :].astype(jnp.float32) for term in (2, 1, 0))
    for head in range(heads):
        other = (head + heads // 2) % heads
        top_a, top_b = here[head : head + 1], there[other : other + 1]
        top = jnp.maximum(top_a, top_b)
        share_a = jnp.exp2((top_a - top) * EXP_SCALE)
        share_b = jnp.exp2((top_b - top) * EXP_SCALE)
        total = here[heads + head : heads + head + 1] * share_a + there[heads + other : heads + other + 1] * share_b
        accum = here_ref[pl.ds(head * HD, HD), :] * share_a
        accum += there_ref[pl.ds(other * HD, HD), :].astype(jnp.float32) * share_b
        att_ref[:, head * HD : (head + 1) * HD] = jnp.transpose(accum / total).astype(jnp.bfloat16)
    for copy in copies:
        copy.wait()
    out_ref[...] = product(att_ref, w_buf, 0)


def project(columns_ref, att_ref, wm_ref, wo_ref, out_ref, w_buf, sems):
    blocks = range(out_ref.shape[0])
    copies = [fetch(columns_ref, block, (wm_ref, wo_ref), w_buf, sems) for block in blocks]
    for copy in sum(copies, []):
        copy.start()
    for block in blocks:
        for copy in copies[block]:
            copy.wait()
        out_ref[block] = product(att_ref, w_buf, block)


VM = pl.BlockSpec(memory_space=pltpu.VMEM)
HBM = pl.BlockSpec(memory_space=pltpu.HBM)
SM = pl.BlockSpec(memory_space=pltpu.SMEM)
LIMIT = pltpu.CompilerParams(vmem_limit_bytes=32 * 1024 * 1024)
WIDE_LIMIT = pltpu.CompilerParams(vmem_limit_bytes=49 * 1024 * 1024)


def on_device(lengths, queries, keys, values, out_weight):
    rows, wide = queries.shape
    units = rows // UNIT
    dp_count, y_count = lax.axis_size("dp"), lax.axis_size("y")
    dp, y, core = lax.axis_index("dp"), lax.axis_index("y"), lax.axis_index("core")
    swap = [(0, 1), (1, 0)]

    own = jnp.concatenate(
        [lax.dynamic_slice_in_dim(keys, y * HD, HD, 1), lax.dynamic_slice_in_dim(values, y * HD, HD, 1)], axis=1
    )
    first_pairs = [
        (2 * i + c, 2 * (i + FIRST_BACK[c]) + c) for c in range(2) for i in range(dp_count - FIRST_BACK[c])
    ]
    first = lax.ppermute(own, ("dp", "core"), first_pairs)
    q_other = lax.ppermute(queries, "core", swap)
    second = lax.ppermute(first, "dp", [(i, i + 1) for i in range(dp_count - 1)])

    w_other = lax.ppermute(out_weight, "core", swap)

    order = jnp.arange(lengths.shape[0], dtype=jnp.int32)
    ends = jnp.sum(jnp.where(order[None, :] <= order[:, None], lengths[None, :], 0), axis=1)
    q_starts = dp * rows + UNIT * jnp.arange(units, dtype=jnp.int32)
    doc_starts = jnp.max(jnp.where(ends[None, :] <= q_starts[:, None], ends[None, :], 0), axis=1)
    lows = doc_starts // UNIT - dp * units
    tail = jnp.stack([1 + 2 * core, 2 + 2 * core, core])
    info = jnp.concatenate([lows, tail]).astype(jnp.int32)

    state_shape = jax.ShapeDtypeStruct((2 * wide + 16, rows), jnp.float32)
    state = pl.pallas_call(
        attend_own,
        out_shape=[state_shape],
        in_specs=[SM, VM, VM, VM],
        out_specs=[VM],
        compiler_params=LIMIT,
        cost_estimate=pl.CostEstimate(flops=OWN_FLOPS, bytes_accessed=4_000_000, transcendentals=1_000_000),
    )(info, queries, q_other, own)
    message_shape = jax.ShapeDtypeStruct((2 * wide + 48, rows), jnp.bfloat16)
    for which, piece in enumerate((first, second)):
        state = pl.pallas_call(
            functools.partial(attend_piece, which),
            out_shape=[state_shape, message_shape][: which + 1],
            in_specs=[SM, VM, VM, VM, VM],
            out_specs=[VM, VM][: which + 1],
            compiler_params=LIMIT,
            cost_estimate=pl.CostEstimate(flops=PIECE_FLOPS[which], bytes_accessed=6_000_000, transcendentals=1_000_000),
        )(info, queries, q_other, piece, state[0])
    state, message = state
    there = lax.ppermute(message, "core", swap)
    half = y_count // 2
    way = 1 - 2 * core

    def columns_at(distance):
        chunk = jnp.mod(y + way * distance, y_count)
        return jnp.stack([2 * chunk + core, 2 * chunk + 1 - core]).astype(jnp.int32)

    def w_scratch(count):
        return [pltpu.VMEM((count, 2 * wide, wide), jnp.bfloat16), pltpu.SemaphoreType.DMA((count, 2))]

    attended, farthest = pl.pallas_call(
        combine,
        out_shape=[
            jax.ShapeDtypeStruct((rows, 2 * wide), jnp.bfloat16),
            jax.ShapeDtypeStruct((rows, wide), jnp.bfloat16),
        ],
        in_specs=[SM, VM, VM, HBM, HBM],
        out_specs=[VM, VM],
        scratch_shapes=w_scratch(1),
        compiler_params=WIDE_LIMIT,
        cost_estimate=pl.CostEstimate(flops=400_000_000, bytes_accessed=5_000_000, transcendentals=10_000),
    )(columns_at(half)[:1], state, there, out_weight, w_other)

    others = jnp.concatenate([*(columns_at(distance) for distance in range(half - 1, 0, -1)), columns_at(0)[:1]])
    count = 2 * half - 1
    parts = pl.pallas_call(
        project,
        out_shape=jax.ShapeDtypeStruct((count, rows, wide), jnp.bfloat16),
        in_specs=[SM, VM, HBM, HBM],
        out_specs=VM,
        scratch_shapes=w_scratch(count),
        compiler_params=WIDE_LIMIT,
        cost_estimate=pl.CostEstimate(flops=PROJECT_FLOPS, bytes_accessed=10_000_000, transcendentals=0),
    )(others, attended, out_weight, w_other)

    straight = [(2 * i + c, 2 * ((i + 1 - 2 * c) % y_count) + c) for i in range(y_count) for c in range(2)]
    cross = [(2 * i + c, 2 * ((i + 1 - 2 * c) % y_count) + 1 - c) for i in range(y_count) for c in range(2)]
    axes = ("y", "core")
    size = rows // ROW_PARTS

    def add(a, *others):
        total = a.astype(jnp.float32)
        for b in others:
            total = total + b.astype(jnp.float32)
        return total.astype(jnp.bfloat16)

    spots = [slice(r * size, (r + 1) * size) for r in range(ROW_PARTS)]
    got = []
    for at in spots:
        value = lax.ppermute(farthest[at], axes, straight)
        got.append(lax.pad(value[None], jnp.zeros((), value.dtype), ((0, 1, 0), (0, 0, 0), (0, 0, 0))))
    token = None
    for distance in range(half - 1, 0, -1):
        first_at = 2 * (half - 1 - distance)
        for r, at in enumerate(spots):
            if token is not None:
                parts, token = lax.optimization_barrier((parts, token))
            now = parts[first_at : first_at + 2, at]
            if distance > 1:
                token = add(now, got[r])
                got[r] = lax.ppermute(token, axes, straight)
            else:
                near, far = add(now[0], got[r][0]), add(now[1], got[r][1])
                token = near
                got[r] = (lax.ppermute(near, axes, straight), lax.ppermute(far, axes, cross))
    outs = []
    for r, at in enumerate(spots):
        if r > 0:
            parts, outs[-1] = lax.optimization_barrier((parts, outs[-1]))
        outs.append(add(parts[count - 1, at], *got[r]))
    return jnp.concatenate(outs, axis=0) if ROW_PARTS > 1 else outs[0]


def solution(mesh):
    dp_count, tensor_count = mesh.shape["dp"], mesh.shape["tensor"]
    split = Mesh(mesh.devices.reshape(dp_count, tensor_count // 2, 2), ("dp", "y", "core"))
    heads = ("y", "core")
    placed = (P(), P("dp", heads), P("dp", None), P("dp", None), P(heads, None))
    return jax.shard_map(on_device, mesh=split, in_specs=placed, out_specs=P("dp", heads), check_vma=False)
```

```python
import functools
import math

import jax
import jax.numpy as jnp
from jax import lax
from jax.experimental import pallas as pl
from jax.experimental.pallas import tpu as pltpu
from jax.sharding import Mesh, PartitionSpec as P

HD = 128
UNIT = 128
NEG = -1e30
EXP_SCALE = math.log2(math.e) / HD**0.5
AHEAD = 3
OWN_FLOPS = 60_000_000_000
PIECE_FLOPS = (60_000_000_000, 60_000_000_000)
PROJECT_FLOPS = 60_000_000_000
STATS = 8 * HD

FIRST_BACK = (1, 3)
SECOND_BACK = (2, 4)


def block_bias(allowed):
    return jnp.where(allowed, 0.0, NEG).astype(jnp.float32)


def head_pair(q_refs, pair, unit):
    q_ref = q_refs[pair // 2]
    rows = pl.ds(unit * UNIT, UNIT)
    first = (pair % 2) * 2 * HD
    return jnp.concatenate([q_ref[rows, first : first + HD], q_ref[rows, first + HD : first + 2 * HD]], axis=0)


def raw_scores(k_rows, q_pair):
    return lax.dot_general(k_rows, q_pair, (((1,), (1,)), ((), ())), preferred_element_type=jnp.float32)


def weighted(v_columns, weights):
    return jnp.dot(v_columns, weights.astype(jnp.bfloat16), preferred_element_type=jnp.float32)


def ahead(steps, compute):
    pending = [compute(*step) for step in steps[:AHEAD]]
    for at, step in enumerate(steps):
        if at + AHEAD < len(steps):
            pending.append(compute(*steps[at + AHEAD]))
        yield step, pending.pop(0)


def store_state(out_ref, pair, unit, top, total, accum):
    heads = 8
    cols = pl.ds(unit * UNIT, UNIT)
    for side in range(2):
        head = 2 * pair + side
        part = slice(side * UNIT, (side + 1) * UNIT)
        out_ref[pl.ds(head * HD, HD), cols] = accum[:, part]
        out_ref[pl.ds(heads * HD + head, 1), cols] = top[:, part]
        out_ref[pl.ds(heads * HD + heads + head, 1), cols] = total[:, part]


def load_state(ref, pair, unit):
    heads = 8
    cols = pl.ds(unit * UNIT, UNIT)
    both = []
    for base, size in ((heads * HD, 1), (heads * HD + heads, 1), (0, HD)):
        halves = [ref[pl.ds(base + (2 * pair + side) * size, size), cols] for side in range(2)]
        both.append(jnp.concatenate(halves, axis=1))
    return both


def piece_bias(info_ref, unit, back, units):
    low = info_ref[unit]
    return [block_bias(low <= block - units * back) for block in range(units)]


def attend_own(info_ref, qm_ref, qo_ref, own_ref, out_ref):
    units = qm_ref.shape[0] // UNIT
    core = info_ref[units + 2]
    triangle = lax.broadcasted_iota(jnp.int32, (UNIT, 2 * UNIT), 0) <= (
        lax.broadcasted_iota(jnp.int32, (UNIT, 2 * UNIT), 1) % UNIT
    )
    v_own = jnp.transpose(own_ref[:, HD:])

    def scores_of(unit, pair):
        return raw_scores(own_ref[: (unit + 1) * UNIT, :HD], head_pair((qm_ref, qo_ref), pair, unit))

    steps = [(unit, pair) for unit in range(units) for pair in range(4)]
    for (unit, pair), raw in ahead(steps, scores_of):
        low = info_ref[unit]
        blocks = []
        for b in range(unit + 1):
            block = raw[b * UNIT : (b + 1) * UNIT] + block_bias((low <= b) & (core == 0))
            blocks.append(jnp.where(triangle, block, NEG) if b == unit else block)
        scores = jnp.concatenate(blocks, axis=0)
        top = jnp.max(scores, axis=0, keepdims=True)
        weights = jnp.exp2((scores - top) * EXP_SCALE)
        total = jnp.sum(weights, axis=0, keepdims=True)
        store_state(out_ref, pair, unit, top, total, weighted(v_own[:, : (unit + 1) * UNIT], weights))


def attend_piece(which, info_ref, qm_ref, qo_ref, piece_ref, state_ref, out_ref, message_ref=None):
    units = qm_ref.shape[0] // UNIT
    v_piece = jnp.transpose(piece_ref[:, HD:])

    def scores_of(unit, pair):
        return raw_scores(piece_ref[:, :HD], head_pair((qm_ref, qo_ref), pair, unit))

    steps = [(unit, pair) for unit in range(units) for pair in range(4)]
    for (unit, pair), raw in ahead(steps, scores_of):
        bias = piece_bias(info_ref, unit, info_ref[units + which], units)
        scores = jnp.concatenate([raw[b * UNIT : (b + 1) * UNIT] + bias[b] for b in range(units)], axis=0)
        old_top, old_total, old_accum = load_state(state_ref, pair, unit)
        top = jnp.maximum(old_top, jnp.max(scores, axis=0, keepdims=True))
        weights = jnp.exp2((scores - top) * EXP_SCALE)
        factor = jnp.exp2((old_top - top) * EXP_SCALE)
        total = old_total * factor + jnp.sum(weights, axis=0, keepdims=True)
        accum = old_accum * factor + weighted(v_piece, weights)
        store_state(out_ref, pair, unit, top, total, accum)
        if message_ref is not None:
            for side in range(2):
                at = pl.ds((2 * pair + side) * HD, HD), pl.ds(unit * UNIT, UNIT)
                message_ref[at] = accum[:, side * UNIT : (side + 1) * UNIT].astype(jnp.bfloat16)
    if message_ref is not None:
        rest = out_ref[STATS:, :]
        for term in range(3):
            rounded = rest.astype(jnp.bfloat16)
            message_ref[pl.ds(STATS + 16 * term, 16), :] = rounded
            rest = rest - rounded.astype(jnp.float32)


def fetch(columns_ref, block, w_refs, w_buf, sems):
    depth, wide = w_buf.shape[1] // 2, w_buf.shape[2]
    at = pl.ds(pl.multiple_of(columns_ref[block] * wide, wide), wide)
    return [
        pltpu.make_async_copy(ref.at[:, at], w_buf.at[block, pl.ds(n * depth, depth)], sems.at[block, n])
        for n, ref in enumerate(w_refs)
    ]


def product(att_ref, w_buf, block):
    return jnp.dot(att_ref[...], w_buf[block], preferred_element_type=jnp.float32).astype(jnp.bfloat16)


def combine(columns_ref, here_ref, there_ref, wm_ref, wo_ref, att_ref, out_ref, w_buf, sems):
    heads = 8
    copies = fetch(columns_ref, 0, (wm_ref, wo_ref), w_buf, sems)
    for copy in copies:
        copy.start()
    here = here_ref[STATS:, :]
    there = sum(there_ref[pl.ds(STATS + 16 * term, 16), :].astype(jnp.float32) for term in (2, 1, 0))
    for head in range(heads):
        other = (head + heads // 2) % heads
        top_a, top_b = here[head : head + 1], there[other : other + 1]
        top = jnp.maximum(top_a, top_b)
        share_a = jnp.exp2((top_a - top) * EXP_SCALE)
        share_b = jnp.exp2((top_b - top) * EXP_SCALE)
        total = here[heads + head : heads + head + 1] * share_a + there[heads + other : heads + other + 1] * share_b
        accum = here_ref[pl.ds(head * HD, HD), :] * share_a
        accum += there_ref[pl.ds(other * HD, HD), :].astype(jnp.float32) * share_b
        att_ref[:, head * HD : (head + 1) * HD] = jnp.transpose(accum / total).astype(jnp.bfloat16)
    for copy in copies:
        copy.wait()
    out_ref[...] = product(att_ref, w_buf, 0)


def project(count, columns_ref, att_ref, wm_ref, wo_ref, *rest):
    out_refs, (w_buf, sems) = rest[:count], rest[count:]
    copies = [fetch(columns_ref, block, (wm_ref, wo_ref), w_buf, sems) for block in range(count)]
    for copy in sum(copies, []):
        copy.start()
    for block in range(count):
        for copy in copies[block]:
            copy.wait()
        out_refs[block][...] = product(att_ref, w_buf, block)


VM = pl.BlockSpec(memory_space=pltpu.VMEM)
HBM = pl.BlockSpec(memory_space=pltpu.HBM)
SM = pl.BlockSpec(memory_space=pltpu.SMEM)
LIMIT = pltpu.CompilerParams(vmem_limit_bytes=32 * 1024 * 1024)
WIDE_LIMIT = pltpu.CompilerParams(vmem_limit_bytes=49 * 1024 * 1024)


def on_device(lengths, queries, keys, values, out_weight):
    rows, wide = queries.shape
    units = rows // UNIT
    dp_count, y_count = lax.axis_size("dp"), lax.axis_size("y")
    dp, y, core = lax.axis_index("dp"), lax.axis_index("y"), lax.axis_index("core")
    swap = [(0, 1), (1, 0)]

    own = jnp.concatenate(
        [lax.dynamic_slice_in_dim(keys, y * HD, HD, 1), lax.dynamic_slice_in_dim(values, y * HD, HD, 1)], axis=1
    )
    first_pairs = [
        (2 * i + c, 2 * (i + FIRST_BACK[c]) + c) for c in range(2) for i in range(dp_count - FIRST_BACK[c])
    ]
    first = lax.ppermute(own, ("dp", "core"), first_pairs)
    q_other = lax.ppermute(queries, "core", swap)
    second = lax.ppermute(first, "dp", [(i, i + 1) for i in range(dp_count - 1)])

    w_other = lax.ppermute(out_weight, "core", swap)

    order = jnp.arange(lengths.shape[0], dtype=jnp.int32)
    ends = jnp.sum(jnp.where(order[None, :] <= order[:, None], lengths[None, :], 0), axis=1)
    q_starts = dp * rows + UNIT * jnp.arange(units, dtype=jnp.int32)
    doc_starts = jnp.max(jnp.where(ends[None, :] <= q_starts[:, None], ends[None, :], 0), axis=1)
    lows = doc_starts // UNIT - dp * units
    tail = jnp.stack([1 + 2 * core, 2 + 2 * core, core])
    info = jnp.concatenate([lows, tail]).astype(jnp.int32)

    state_shape = jax.ShapeDtypeStruct((2 * wide + 16, rows), jnp.float32)
    state = pl.pallas_call(
        attend_own,
        out_shape=[state_shape],
        in_specs=[SM, VM, VM, VM],
        out_specs=[VM],
        compiler_params=LIMIT,
        cost_estimate=pl.CostEstimate(flops=OWN_FLOPS, bytes_accessed=4_000_000, transcendentals=1_000_000),
    )(info, queries, q_other, own)
    message_shape = jax.ShapeDtypeStruct((2 * wide + 48, rows), jnp.bfloat16)
    for which, piece in enumerate((first, second)):
        state = pl.pallas_call(
            functools.partial(attend_piece, which),
            out_shape=[state_shape, message_shape][: which + 1],
            in_specs=[SM, VM, VM, VM, VM],
            out_specs=[VM, VM][: which + 1],
            compiler_params=LIMIT,
            cost_estimate=pl.CostEstimate(flops=PIECE_FLOPS[which], bytes_accessed=6_000_000, transcendentals=1_000_000),
        )(info, queries, q_other, piece, state[0])
    state, message = state
    there = lax.ppermute(message, "core", swap)
    half = y_count // 2
    way = 1 - 2 * core

    def columns_at(distance):
        chunk = jnp.mod(y + way * distance, y_count)
        return jnp.stack([2 * chunk + core, 2 * chunk + 1 - core]).astype(jnp.int32)

    def w_scratch(count):
        return [pltpu.VMEM((count, 2 * wide, wide), jnp.bfloat16), pltpu.SemaphoreType.DMA((count, 2))]

    attended, farthest = pl.pallas_call(
        combine,
        out_shape=[
            jax.ShapeDtypeStruct((rows, 2 * wide), jnp.bfloat16),
            jax.ShapeDtypeStruct((rows, wide), jnp.bfloat16),
        ],
        in_specs=[SM, VM, VM, HBM, HBM],
        out_specs=[VM, VM],
        scratch_shapes=w_scratch(1),
        compiler_params=WIDE_LIMIT,
        cost_estimate=pl.CostEstimate(flops=400_000_000, bytes_accessed=5_000_000, transcendentals=10_000),
    )(columns_at(half)[:1], state, there, out_weight, w_other)

    def part(columns):
        count = columns.shape[0]
        return pl.pallas_call(
            functools.partial(project, count),
            out_shape=[jax.ShapeDtypeStruct((rows, wide), jnp.bfloat16)] * count,
            in_specs=[SM, VM, HBM, HBM],
            out_specs=[VM] * count,
            scratch_shapes=w_scratch(count),
            compiler_params=WIDE_LIMIT,
            cost_estimate=pl.CostEstimate(flops=PROJECT_FLOPS, bytes_accessed=10_000_000, transcendentals=0),
        )(columns, attended, out_weight, w_other)

    straight = [(2 * i + c, 2 * ((i + 1 - 2 * c) % y_count) + c) for i in range(y_count) for c in range(2)]
    cross = [(2 * i + c, 2 * ((i + 1 - 2 * c) % y_count) + 1 - c) for i in range(y_count) for c in range(2)]
    axes = ("y", "core")

    def add(a, *others):
        total = a.astype(jnp.float32)
        for b in others:
            total = total + b.astype(jnp.float32)
        return total.astype(jnp.bfloat16)

    near = lax.ppermute(farthest, axes, straight)
    now = part(columns_at(half - 1))
    far = lax.ppermute(now[1], axes, straight)
    for distance in range(half - 1, 0, -1):
        send = add(now[0], near)
        near = lax.ppermute(send, axes, straight)
        if distance > 1:
            now = part(columns_at(distance - 1))
            now, send = lax.optimization_barrier((now, send))
            send = add(now[1], far)
            far = lax.ppermute(send, axes, straight if distance > 2 else cross)
            now, send = lax.optimization_barrier((now, send))
    mine = part(columns_at(0)[:1])[0]
    return add(mine, near, far)


def solution(mesh):
    dp_count, tensor_count = mesh.shape["dp"], mesh.shape["tensor"]
    split = Mesh(mesh.devices.reshape(dp_count, tensor_count // 2, 2), ("dp", "y", "core"))
    heads = ("y", "core")
    placed = (P(), P("dp", heads), P("dp", None), P("dp", None), P(heads, None))
    return jax.shard_map(on_device, mesh=split, in_specs=placed, out_specs=P("dp", heads), check_vma=False)
```

```python
import functools
import math

import jax
import jax.numpy as jnp
from jax import lax
from jax.experimental import pallas as pl
from jax.experimental.pallas import tpu as pltpu
from jax.sharding import Mesh, PartitionSpec as P

HD = 128
UNIT = 128
NEG = -1e30
EXP_SCALE = math.log2(math.e) / HD**0.5
AHEAD = 3
OWN_FLOPS = 60_000_000_000
PIECE_FLOPS = (60_000_000_000, 60_000_000_000)
PROJECT_FLOPS = 60_000_000_000
STATS = 8 * HD

FIRST_BACK = (1, 3)
SECOND_BACK = (2, 4)


def block_bias(allowed):
    return jnp.where(allowed, 0.0, NEG).astype(jnp.float32)


def head_pair(q_refs, pair, unit):
    q_ref = q_refs[pair // 2]
    rows = pl.ds(unit * UNIT, UNIT)
    first = (pair % 2) * 2 * HD
    return jnp.concatenate([q_ref[rows, first : first + HD], q_ref[rows, first + HD : first + 2 * HD]], axis=0)


def raw_scores(k_rows, q_pair):
    return lax.dot_general(k_rows, q_pair, (((1,), (1,)), ((), ())), preferred_element_type=jnp.float32)


def weighted(v_columns, weights):
    return jnp.dot(v_columns, weights.astype(jnp.bfloat16), preferred_element_type=jnp.float32)


def ahead(steps, compute):
    pending = [compute(*step) for step in steps[:AHEAD]]
    for at, step in enumerate(steps):
        if at + AHEAD < len(steps):
            pending.append(compute(*steps[at + AHEAD]))
        yield step, pending.pop(0)


def store_state(out_ref, pair, unit, top, total, accum):
    heads = 8
    cols = pl.ds(unit * UNIT, UNIT)
    for side in range(2):
        head = 2 * pair + side
        part = slice(side * UNIT, (side + 1) * UNIT)
        out_ref[pl.ds(head * HD, HD), cols] = accum[:, part]
        out_ref[pl.ds(heads * HD + head, 1), cols] = top[:, part]
        out_ref[pl.ds(heads * HD + heads + head, 1), cols] = total[:, part]


def load_state(ref, pair, unit):
    heads = 8
    cols = pl.ds(unit * UNIT, UNIT)
    both = []
    for base, size in ((heads * HD, 1), (heads * HD + heads, 1), (0, HD)):
        halves = [ref[pl.ds(base + (2 * pair + side) * size, size), cols] for side in range(2)]
        both.append(jnp.concatenate(halves, axis=1))
    return both


def piece_bias(info_ref, unit, back, units):
    low = info_ref[unit]
    return [block_bias(low <= block - units * back) for block in range(units)]


def attend_own(info_ref, qm_ref, qo_ref, own_ref, out_ref):
    units = qm_ref.shape[0] // UNIT
    core = info_ref[units + 2]
    triangle = lax.broadcasted_iota(jnp.int32, (UNIT, 2 * UNIT), 0) <= (
        lax.broadcasted_iota(jnp.int32, (UNIT, 2 * UNIT), 1) % UNIT
    )
    v_own = jnp.transpose(own_ref[:, HD:])

    def scores_of(unit, pair):
        return raw_scores(own_ref[: (unit + 1) * UNIT, :HD], head_pair((qm_ref, qo_ref), pair, unit))

    steps = [(unit, pair) for unit in range(units) for pair in range(4)]
    for (unit, pair), raw in ahead(steps, scores_of):
        low = info_ref[unit]
        blocks = []
        for b in range(unit + 1):
            block = raw[b * UNIT : (b + 1) * UNIT] + block_bias((low <= b) & (core == 0))
            blocks.append(jnp.where(triangle, block, NEG) if b == unit else block)
        scores = jnp.concatenate(blocks, axis=0)
        top = jnp.max(scores, axis=0, keepdims=True)
        weights = jnp.exp2((scores - top) * EXP_SCALE)
        total = jnp.sum(weights, axis=0, keepdims=True)
        store_state(out_ref, pair, unit, top, total, weighted(v_own[:, : (unit + 1) * UNIT], weights))


def attend_piece(which, info_ref, qm_ref, qo_ref, piece_ref, state_ref, out_ref, message_ref=None):
    units = qm_ref.shape[0] // UNIT
    v_piece = jnp.transpose(piece_ref[:, HD:])

    def scores_of(unit, pair):
        return raw_scores(piece_ref[:, :HD], head_pair((qm_ref, qo_ref), pair, unit))

    steps = [(unit, pair) for unit in range(units) for pair in range(4)]
    for (unit, pair), raw in ahead(steps, scores_of):
        bias = piece_bias(info_ref, unit, info_ref[units + which], units)
        scores = jnp.concatenate([raw[b * UNIT : (b + 1) * UNIT] + bias[b] for b in range(units)], axis=0)
        old_top, old_total, old_accum = load_state(state_ref, pair, unit)
        top = jnp.maximum(old_top, jnp.max(scores, axis=0, keepdims=True))
        weights = jnp.exp2((scores - top) * EXP_SCALE)
        factor = jnp.exp2((old_top - top) * EXP_SCALE)
        total = old_total * factor + jnp.sum(weights, axis=0, keepdims=True)
        accum = old_accum * factor + weighted(v_piece, weights)
        store_state(out_ref, pair, unit, top, total, accum)
        if message_ref is not None:
            for side in range(2):
                at = pl.ds((2 * pair + side) * HD, HD), pl.ds(unit * UNIT, UNIT)
                message_ref[at] = accum[:, side * UNIT : (side + 1) * UNIT].astype(jnp.bfloat16)
    if message_ref is not None:
        rest = out_ref[STATS:, :]
        for term in range(3):
            rounded = rest.astype(jnp.bfloat16)
            message_ref[pl.ds(STATS + 16 * term, 16), :] = rounded
            rest = rest - rounded.astype(jnp.float32)


def fetch(columns_ref, block, w_refs, w_buf, sems):
    depth, wide = w_buf.shape[1] // 2, w_buf.shape[2]
    at = pl.ds(pl.multiple_of(columns_ref[block] * wide, wide), wide)
    return [
        pltpu.make_async_copy(ref.at[:, at], w_buf.at[block, pl.ds(n * depth, depth)], sems.at[block, n])
        for n, ref in enumerate(w_refs)
    ]


def product(att_ref, w_buf, block):
    return jnp.dot(att_ref[...], w_buf[block], preferred_element_type=jnp.float32).astype(jnp.bfloat16)


def combine(columns_ref, here_ref, there_ref, wm_ref, wo_ref, att_ref, out_ref, w_buf, sems):
    heads = 8
    copies = fetch(columns_ref, 0, (wm_ref, wo_ref), w_buf, sems)
    for copy in copies:
        copy.start()
    here = here_ref[STATS:, :]
    there = sum(there_ref[pl.ds(STATS + 16 * term, 16), :].astype(jnp.float32) for term in (2, 1, 0))
    for head in range(heads):
        other = (head + heads // 2) % heads
        top_a, top_b = here[head : head + 1], there[other : other + 1]
        top = jnp.maximum(top_a, top_b)
        share_a = jnp.exp2((top_a - top) * EXP_SCALE)
        share_b = jnp.exp2((top_b - top) * EXP_SCALE)
        total = here[heads + head : heads + head + 1] * share_a + there[heads + other : heads + other + 1] * share_b
        accum = here_ref[pl.ds(head * HD, HD), :] * share_a
        accum += there_ref[pl.ds(other * HD, HD), :].astype(jnp.float32) * share_b
        att_ref[:, head * HD : (head + 1) * HD] = jnp.transpose(accum / total).astype(jnp.bfloat16)
    for copy in copies:
        copy.wait()
    out_ref[...] = product(att_ref, w_buf, 0)


def project(count, columns_ref, att_ref, wm_ref, wo_ref, *rest):
    out_refs, (w_buf, sems) = rest[:count], rest[count:]
    copies = [fetch(columns_ref, block, (wm_ref, wo_ref), w_buf, sems) for block in range(count)]
    for copy in sum(copies, []):
        copy.start()
    for block in range(count):
        for copy in copies[block]:
            copy.wait()
        out_refs[block][...] = product(att_ref, w_buf, block)


VM = pl.BlockSpec(memory_space=pltpu.VMEM)
HBM = pl.BlockSpec(memory_space=pltpu.HBM)
SM = pl.BlockSpec(memory_space=pltpu.SMEM)
LIMIT = pltpu.CompilerParams(vmem_limit_bytes=32 * 1024 * 1024)
WIDE_LIMIT = pltpu.CompilerParams(vmem_limit_bytes=49 * 1024 * 1024)


def on_device(lengths, queries, keys, values, out_weight):
    rows, wide = queries.shape
    units = rows // UNIT
    dp_count, y_count = lax.axis_size("dp"), lax.axis_size("y")
    dp, y, core = lax.axis_index("dp"), lax.axis_index("y"), lax.axis_index("core")
    swap = [(0, 1), (1, 0)]

    own = jnp.concatenate(
        [lax.dynamic_slice_in_dim(keys, y * HD, HD, 1), lax.dynamic_slice_in_dim(values, y * HD, HD, 1)], axis=1
    )
    first_pairs = [
        (2 * i + c, 2 * (i + FIRST_BACK[c]) + c) for c in range(2) for i in range(dp_count - FIRST_BACK[c])
    ]
    first = lax.ppermute(own, ("dp", "core"), first_pairs)
    own, q_sent = lax.optimization_barrier((own, queries))
    q_other = lax.ppermute(q_sent, "core", swap)
    second = lax.ppermute(first, "dp", [(i, i + 1) for i in range(dp_count - 1)])

    w_other = lax.ppermute(out_weight, "core", swap)

    order = jnp.arange(lengths.shape[0], dtype=jnp.int32)
    ends = jnp.sum(jnp.where(order[None, :] <= order[:, None], lengths[None, :], 0), axis=1)
    q_starts = dp * rows + UNIT * jnp.arange(units, dtype=jnp.int32)
    doc_starts = jnp.max(jnp.where(ends[None, :] <= q_starts[:, None], ends[None, :], 0), axis=1)
    lows = doc_starts // UNIT - dp * units
    tail = jnp.stack([1 + 2 * core, 2 + 2 * core, core])
    info = jnp.concatenate([lows, tail]).astype(jnp.int32)

    state_shape = jax.ShapeDtypeStruct((2 * wide + 16, rows), jnp.float32)
    state = pl.pallas_call(
        attend_own,
        out_shape=[state_shape],
        in_specs=[SM, VM, VM, VM],
        out_specs=[VM],
        compiler_params=LIMIT,
        cost_estimate=pl.CostEstimate(flops=OWN_FLOPS, bytes_accessed=4_000_000, transcendentals=1_000_000),
    )(info, queries, q_other, own)
    message_shape = jax.ShapeDtypeStruct((2 * wide + 48, rows), jnp.bfloat16)
    for which, piece in enumerate((first, second)):
        state = pl.pallas_call(
            functools.partial(attend_piece, which),
            out_shape=[state_shape, message_shape][: which + 1],
            in_specs=[SM, VM, VM, VM, VM],
            out_specs=[VM, VM][: which + 1],
            compiler_params=LIMIT,
            cost_estimate=pl.CostEstimate(flops=PIECE_FLOPS[which], bytes_accessed=6_000_000, transcendentals=1_000_000),
        )(info, queries, q_other, piece, state[0])
    state, message = state
    there = lax.ppermute(message, "core", swap)
    half = y_count // 2
    way = 1 - 2 * core

    def columns_at(distance):
        chunk = jnp.mod(y + way * distance, y_count)
        return jnp.stack([2 * chunk + core, 2 * chunk + 1 - core]).astype(jnp.int32)

    def w_scratch(count):
        return [pltpu.VMEM((count, 2 * wide, wide), jnp.bfloat16), pltpu.SemaphoreType.DMA((count, 2))]

    attended, farthest = pl.pallas_call(
        combine,
        out_shape=[
            jax.ShapeDtypeStruct((rows, 2 * wide), jnp.bfloat16),
            jax.ShapeDtypeStruct((rows, wide), jnp.bfloat16),
        ],
        in_specs=[SM, VM, VM, HBM, HBM],
        out_specs=[VM, VM],
        scratch_shapes=w_scratch(1),
        compiler_params=WIDE_LIMIT,
        cost_estimate=pl.CostEstimate(flops=400_000_000, bytes_accessed=5_000_000, transcendentals=10_000),
    )(columns_at(half)[:1], state, there, out_weight, w_other)

    def part(columns):
        count = columns.shape[0]
        return pl.pallas_call(
            functools.partial(project, count),
            out_shape=[jax.ShapeDtypeStruct((rows, wide), jnp.bfloat16)] * count,
            in_specs=[SM, VM, HBM, HBM],
            out_specs=[VM] * count,
            scratch_shapes=w_scratch(count),
            compiler_params=WIDE_LIMIT,
            cost_estimate=pl.CostEstimate(flops=PROJECT_FLOPS, bytes_accessed=10_000_000, transcendentals=0),
        )(columns, attended, out_weight, w_other)

    straight = [(2 * i + c, 2 * ((i + 1 - 2 * c) % y_count) + c) for i in range(y_count) for c in range(2)]
    cross = [(2 * i + c, 2 * ((i + 1 - 2 * c) % y_count) + 1 - c) for i in range(y_count) for c in range(2)]
    axes = ("y", "core")

    def add(a, *others):
        total = a.astype(jnp.float32)
        for b in others:
            total = total + b.astype(jnp.float32)
        return total.astype(jnp.bfloat16)

    near = lax.ppermute(farthest, axes, straight)
    now = part(columns_at(half - 1))
    far = lax.ppermute(now[1], axes, straight)
    rest = part(jnp.concatenate([*(columns_at(distance) for distance in range(half - 2, 0, -1)), columns_at(0)[:1]]))
    for distance in range(half - 1, 0, -1):
        send = add(now[0], near)
        near = lax.ppermute(send, axes, straight)
        if distance > 1:
            rest, send = lax.optimization_barrier((rest, send))
            now, rest = rest[:2], rest[2:]
            send = add(now[1], far)
            far = lax.ppermute(send, axes, straight if distance > 2 else cross)
            now, send = lax.optimization_barrier((now, send))
    return add(rest[0], near, far)


def solution(mesh):
    dp_count, tensor_count = mesh.shape["dp"], mesh.shape["tensor"]
    split = Mesh(mesh.devices.reshape(dp_count, tensor_count // 2, 2), ("dp", "y", "core"))
    heads = ("y", "core")
    placed = (P(), P("dp", heads), P("dp", None), P("dp", None), P(heads, None))
    return jax.shard_map(on_device, mesh=split, in_specs=placed, out_specs=P("dp", heads), check_vma=False)
```

```python
import functools
import math

import jax
import jax.numpy as jnp
from jax import lax
from jax.experimental import pallas as pl
from jax.experimental.pallas import tpu as pltpu
from jax.sharding import Mesh, PartitionSpec as P

HD = 128
UNIT = 128
NEG = -1e30
EXP_SCALE = math.log2(math.e) / HD**0.5
AHEAD = 3
OWN_FLOPS = 60_000_000_000
PIECE_FLOPS = (60_000_000_000, 60_000_000_000)
PROJECT_FLOPS = 60_000_000_000
STATS = 8 * HD

FIRST_BACK = (1, 3)
SECOND_BACK = (2, 4)


def block_bias(allowed):
    return jnp.where(allowed, 0.0, NEG).astype(jnp.float32)


def head_pair(q_refs, pair, unit):
    q_ref = q_refs[pair // 2]
    rows = pl.ds(unit * UNIT, UNIT)
    first = (pair % 2) * 2 * HD
    return jnp.concatenate([q_ref[rows, first : first + HD], q_ref[rows, first + HD : first + 2 * HD]], axis=0)


def raw_scores(k_rows, q_pair):
    return lax.dot_general(k_rows, q_pair, (((1,), (1,)), ((), ())), preferred_element_type=jnp.float32)


def weighted(v_columns, weights):
    return jnp.dot(v_columns, weights.astype(jnp.bfloat16), preferred_element_type=jnp.float32)


def ahead(steps, compute):
    pending = [compute(*step) for step in steps[:AHEAD]]
    for at, step in enumerate(steps):
        if at + AHEAD < len(steps):
            pending.append(compute(*steps[at + AHEAD]))
        yield step, pending.pop(0)


def store_state(out_ref, pair, unit, top, total, accum):
    heads = 8
    cols = pl.ds(unit * UNIT, UNIT)
    for side in range(2):
        head = 2 * pair + side
        part = slice(side * UNIT, (side + 1) * UNIT)
        out_ref[pl.ds(head * HD, HD), cols] = accum[:, part]
        out_ref[pl.ds(heads * HD + head, 1), cols] = top[:, part]
        out_ref[pl.ds(heads * HD + heads + head, 1), cols] = total[:, part]


def load_state(ref, pair, unit):
    heads = 8
    cols = pl.ds(unit * UNIT, UNIT)
    both = []
    for base, size in ((heads * HD, 1), (heads * HD + heads, 1), (0, HD)):
        halves = [ref[pl.ds(base + (2 * pair + side) * size, size), cols] for side in range(2)]
        both.append(jnp.concatenate(halves, axis=1))
    return both


def piece_bias(info_ref, unit, back, units):
    low = info_ref[unit]
    return [block_bias(low <= block - units * back) for block in range(units)]


def attend_own(info_ref, qm_ref, qo_ref, own_ref, out_ref):
    units = qm_ref.shape[0] // UNIT
    core = info_ref[units + 2]
    triangle = lax.broadcasted_iota(jnp.int32, (UNIT, 2 * UNIT), 0) <= (
        lax.broadcasted_iota(jnp.int32, (UNIT, 2 * UNIT), 1) % UNIT
    )
    v_own = jnp.transpose(own_ref[:, HD:])

    def scores_of(unit, pair):
        return raw_scores(own_ref[: (unit + 1) * UNIT, :HD], head_pair((qm_ref, qo_ref), pair, unit))

    steps = [(unit, pair) for unit in range(units) for pair in range(4)]
    for (unit, pair), raw in ahead(steps, scores_of):
        low = info_ref[unit]
        blocks = []
        for b in range(unit + 1):
            block = raw[b * UNIT : (b + 1) * UNIT] + block_bias((low <= b) & (core == 0))
            blocks.append(jnp.where(triangle, block, NEG) if b == unit else block)
        scores = jnp.concatenate(blocks, axis=0)
        top = jnp.max(scores, axis=0, keepdims=True)
        weights = jnp.exp2((scores - top) * EXP_SCALE)
        total = jnp.sum(weights, axis=0, keepdims=True)
        store_state(out_ref, pair, unit, top, total, weighted(v_own[:, : (unit + 1) * UNIT], weights))


def attend_piece(which, info_ref, qm_ref, qo_ref, piece_ref, state_ref, out_ref, message_ref=None):
    units = qm_ref.shape[0] // UNIT
    v_piece = jnp.transpose(piece_ref[:, HD:])

    def scores_of(unit, pair):
        return raw_scores(piece_ref[:, :HD], head_pair((qm_ref, qo_ref), pair, unit))

    steps = [(unit, pair) for unit in range(units) for pair in range(4)]
    for (unit, pair), raw in ahead(steps, scores_of):
        bias = piece_bias(info_ref, unit, info_ref[units + which], units)
        scores = jnp.concatenate([raw[b * UNIT : (b + 1) * UNIT] + bias[b] for b in range(units)], axis=0)
        old_top, old_total, old_accum = load_state(state_ref, pair, unit)
        top = jnp.maximum(old_top, jnp.max(scores, axis=0, keepdims=True))
        weights = jnp.exp2((scores - top) * EXP_SCALE)
        factor = jnp.exp2((old_top - top) * EXP_SCALE)
        total = old_total * factor + jnp.sum(weights, axis=0, keepdims=True)
        accum = old_accum * factor + weighted(v_piece, weights)
        store_state(out_ref, pair, unit, top, total, accum)
        if message_ref is not None:
            for side in range(2):
                at = pl.ds((2 * pair + side) * HD, HD), pl.ds(unit * UNIT, UNIT)
                message_ref[at] = accum[:, side * UNIT : (side + 1) * UNIT].astype(jnp.bfloat16)
    if message_ref is not None:
        rest = out_ref[STATS:, :]
        for term in range(3):
            rounded = rest.astype(jnp.bfloat16)
            message_ref[pl.ds(STATS + 16 * term, 16), :] = rounded
            rest = rest - rounded.astype(jnp.float32)


def fetch(columns_ref, block, w_refs, w_buf, sems):
    depth, wide = w_buf.shape[1] // 2, w_buf.shape[2]
    at = pl.ds(pl.multiple_of(columns_ref[block] * wide, wide), wide)
    return [
        pltpu.make_async_copy(ref.at[:, at], w_buf.at[block, pl.ds(n * depth, depth)], sems.at[block, n])
        for n, ref in enumerate(w_refs)
    ]


def product(att_ref, w_buf, block):
    return jnp.dot(att_ref[...], w_buf[block], preferred_element_type=jnp.float32).astype(jnp.bfloat16)


def combine(columns_ref, here_ref, there_ref, wm_ref, wo_ref, att_ref, *rest):
    heads = 8
    out_refs, (w_buf, sems) = rest[:-2], rest[-2:]
    copies = [fetch(columns_ref, block, (wm_ref, wo_ref), w_buf, sems) for block in range(len(out_refs))]
    for copy in sum(copies, []):
        copy.start()
    here = here_ref[STATS:, :]
    there = sum(there_ref[pl.ds(STATS + 16 * term, 16), :].astype(jnp.float32) for term in (2, 1, 0))
    for head in range(heads):
        other = (head + heads // 2) % heads
        top_a, top_b = here[head : head + 1], there[other : other + 1]
        top = jnp.maximum(top_a, top_b)
        share_a = jnp.exp2((top_a - top) * EXP_SCALE)
        share_b = jnp.exp2((top_b - top) * EXP_SCALE)
        total = here[heads + head : heads + head + 1] * share_a + there[heads + other : heads + other + 1] * share_b
        accum = here_ref[pl.ds(head * HD, HD), :] * share_a
        accum += there_ref[pl.ds(other * HD, HD), :].astype(jnp.float32) * share_b
        att_ref[:, head * HD : (head + 1) * HD] = jnp.transpose(accum / total).astype(jnp.bfloat16)
    for block, out_ref in enumerate(out_refs):
        for copy in copies[block]:
            copy.wait()
        out_ref[...] = product(att_ref, w_buf, block)


def project(count, columns_ref, att_ref, wm_ref, wo_ref, *rest):
    out_refs, (w_buf, sems) = rest[:count], rest[count:]
    copies = [fetch(columns_ref, block, (wm_ref, wo_ref), w_buf, sems) for block in range(count)]
    for copy in sum(copies, []):
        copy.start()
    for block in range(count):
        for copy in copies[block]:
            copy.wait()
        out_refs[block][...] = product(att_ref, w_buf, block)


VM = pl.BlockSpec(memory_space=pltpu.VMEM)
HBM = pl.BlockSpec(memory_space=pltpu.HBM)
SM = pl.BlockSpec(memory_space=pltpu.SMEM)
LIMIT = pltpu.CompilerParams(vmem_limit_bytes=32 * 1024 * 1024)
WIDE_LIMIT = pltpu.CompilerParams(vmem_limit_bytes=49 * 1024 * 1024)


def on_device(lengths, queries, keys, values, out_weight):
    rows, wide = queries.shape
    units = rows // UNIT
    dp_count, y_count = lax.axis_size("dp"), lax.axis_size("y")
    dp, y, core = lax.axis_index("dp"), lax.axis_index("y"), lax.axis_index("core")
    swap = [(0, 1), (1, 0)]

    own = jnp.concatenate(
        [lax.dynamic_slice_in_dim(keys, y * HD, HD, 1), lax.dynamic_slice_in_dim(values, y * HD, HD, 1)], axis=1
    )
    first_pairs = [
        (2 * i + c, 2 * (i + FIRST_BACK[c]) + c) for c in range(2) for i in range(dp_count - FIRST_BACK[c])
    ]
    first = lax.ppermute(own, ("dp", "core"), first_pairs)
    own, q_sent = lax.optimization_barrier((own, queries))
    q_other = lax.ppermute(q_sent, "core", swap)
    second = lax.ppermute(first, "dp", [(i, i + 1) for i in range(dp_count - 1)])

    w_other = lax.ppermute(out_weight, "core", swap)

    order = jnp.arange(lengths.shape[0], dtype=jnp.int32)
    ends = jnp.sum(jnp.where(order[None, :] <= order[:, None], lengths[None, :], 0), axis=1)
    q_starts = dp * rows + UNIT * jnp.arange(units, dtype=jnp.int32)
    doc_starts = jnp.max(jnp.where(ends[None, :] <= q_starts[:, None], ends[None, :], 0), axis=1)
    lows = doc_starts // UNIT - dp * units
    tail = jnp.stack([1 + 2 * core, 2 + 2 * core, core])
    info = jnp.concatenate([lows, tail]).astype(jnp.int32)

    state_shape = jax.ShapeDtypeStruct((2 * wide + 16, rows), jnp.float32)
    state = pl.pallas_call(
        attend_own,
        out_shape=[state_shape],
        in_specs=[SM, VM, VM, VM],
        out_specs=[VM],
        compiler_params=LIMIT,
        cost_estimate=pl.CostEstimate(flops=OWN_FLOPS, bytes_accessed=4_000_000, transcendentals=1_000_000),
    )(info, queries, q_other, own)
    message_shape = jax.ShapeDtypeStruct((2 * wide + 48, rows), jnp.bfloat16)
    for which, piece in enumerate((first, second)):
        state = pl.pallas_call(
            functools.partial(attend_piece, which),
            out_shape=[state_shape, message_shape][: which + 1],
            in_specs=[SM, VM, VM, VM, VM],
            out_specs=[VM, VM][: which + 1],
            compiler_params=LIMIT,
            cost_estimate=pl.CostEstimate(flops=PIECE_FLOPS[which], bytes_accessed=6_000_000, transcendentals=1_000_000),
        )(info, queries, q_other, piece, state[0])
    state, message = state
    there = lax.ppermute(message, "core", swap)
    half = y_count // 2
    way = 1 - 2 * core

    def columns_at(distance):
        chunk = jnp.mod(y + way * distance, y_count)
        return jnp.stack([2 * chunk + core, 2 * chunk + 1 - core]).astype(jnp.int32)

    def w_scratch(count):
        return [pltpu.VMEM((count, 2 * wide, wide), jnp.bfloat16), pltpu.SemaphoreType.DMA((count, 2))]

    attended, farthest, near, far = pl.pallas_call(
        combine,
        out_shape=[
            jax.ShapeDtypeStruct((rows, 2 * wide), jnp.bfloat16),
            *[jax.ShapeDtypeStruct((rows, wide), jnp.bfloat16)] * 3,
        ],
        in_specs=[SM, VM, VM, HBM, HBM],
        out_specs=[VM] * 4,
        scratch_shapes=w_scratch(3),
        compiler_params=WIDE_LIMIT,
        cost_estimate=pl.CostEstimate(flops=400_000_000, bytes_accessed=5_000_000, transcendentals=10_000),
    )(jnp.concatenate([columns_at(half)[:1], columns_at(half - 1)]), state, there, out_weight, w_other)

    def part(columns):
        count = columns.shape[0]
        return pl.pallas_call(
            functools.partial(project, count),
            out_shape=[jax.ShapeDtypeStruct((rows, wide), jnp.bfloat16)] * count,
            in_specs=[SM, VM, HBM, HBM],
            out_specs=[VM] * count,
            scratch_shapes=w_scratch(count),
            compiler_params=WIDE_LIMIT,
            cost_estimate=pl.CostEstimate(flops=PROJECT_FLOPS, bytes_accessed=10_000_000, transcendentals=0),
        )(columns, attended, out_weight, w_other)

    def carried(hops, crossing):
        return [
            (2 * i + c, 2 * ((i + (1 - 2 * c) * hops) % y_count) + (1 - c if crossing else c))
            for i in range(y_count)
            for c in range(2)
        ]

    straight = carried(1, False)
    axes = ("y", "core")

    def add(a, *others):
        total = a.astype(jnp.float32)
        for b in others:
            total = total + b.astype(jnp.float32)
        return total.astype(jnp.bfloat16)

    joining = [lax.ppermute(farthest, axes, carried(2, False))]
    near = lax.ppermute(near, axes, straight)
    far = lax.ppermute(far, axes, straight)
    rest = part(jnp.concatenate([*(columns_at(distance) for distance in range(half - 2, 0, -1)), columns_at(0)[:1]]))
    for distance in range(half - 2, 0, -1):
        send = add(rest[0], near, *joining)
        joining = []
        near = lax.ppermute(send, axes, straight)
        rest, send = lax.optimization_barrier((rest, send))
        send = add(rest[1], far)
        far = lax.ppermute(send, axes, straight if distance > 1 else carried(1, True))
        rest, send = lax.optimization_barrier((rest[2:], send))
    return add(rest[0], near, far)


def solution(mesh):
    dp_count, tensor_count = mesh.shape["dp"], mesh.shape["tensor"]
    split = Mesh(mesh.devices.reshape(dp_count, tensor_count // 2, 2), ("dp", "y", "core"))
    heads = ("y", "core")
    placed = (P(), P("dp", heads), P("dp", None), P("dp", None), P(heads, None))
    return jax.shard_map(on_device, mesh=split, in_specs=placed, out_specs=P("dp", heads), check_vma=False)
```

```python
import functools
import math

import jax
import jax.numpy as jnp
from jax import lax
from jax.experimental import pallas as pl
from jax.experimental.pallas import tpu as pltpu
from jax.sharding import Mesh, PartitionSpec as P

HD = 128
UNIT = 128
NEG = -1e30
EXP_SCALE = math.log2(math.e) / HD**0.5
AHEAD = 3
OWN_FLOPS = 60_000_000_000
PIECE_FLOPS = (60_000_000_000, 60_000_000_000)
PROJECT_FLOPS = 60_000_000_000
STATS = 8 * HD

FIRST_BACK = (1, 3)
SECOND_BACK = (2, 4)


def block_bias(allowed):
    return jnp.where(allowed, 0.0, NEG).astype(jnp.float32)


def head_pair(q_refs, pair, unit):
    q_ref = q_refs[pair // 2]
    rows = pl.ds(unit * UNIT, UNIT)
    first = (pair % 2) * 2 * HD
    return jnp.concatenate([q_ref[rows, first : first + HD], q_ref[rows, first + HD : first + 2 * HD]], axis=0)


def raw_scores(k_rows, q_pair):
    return lax.dot_general(k_rows, q_pair, (((1,), (1,)), ((), ())), preferred_element_type=jnp.float32)


def weighted(v_columns, weights):
    return jnp.dot(v_columns, weights.astype(jnp.bfloat16), preferred_element_type=jnp.float32)


def ahead(steps, compute):
    pending = [compute(*step) for step in steps[:AHEAD]]
    for at, step in enumerate(steps):
        if at + AHEAD < len(steps):
            pending.append(compute(*steps[at + AHEAD]))
        yield step, pending.pop(0)


def store_state(out_ref, pair, unit, top, total, accum):
    heads = 8
    cols = pl.ds(unit * UNIT, UNIT)
    for side in range(2):
        head = 2 * pair + side
        part = slice(side * UNIT, (side + 1) * UNIT)
        out_ref[pl.ds(head * HD, HD), cols] = accum[:, part]
        out_ref[pl.ds(heads * HD + head, 1), cols] = top[:, part]
        out_ref[pl.ds(heads * HD + heads + head, 1), cols] = total[:, part]


def load_state(ref, pair, unit):
    heads = 8
    cols = pl.ds(unit * UNIT, UNIT)
    both = []
    for base, size in ((heads * HD, 1), (heads * HD + heads, 1), (0, HD)):
        halves = [ref[pl.ds(base + (2 * pair + side) * size, size), cols] for side in range(2)]
        both.append(jnp.concatenate(halves, axis=1))
    return both


def piece_bias(info_ref, unit, back, units):
    low = info_ref[unit]
    return [block_bias(low <= block - units * back) for block in range(units)]


def attend_own(info_ref, qm_ref, qo_ref, own_ref, out_ref):
    units = qm_ref.shape[0] // UNIT
    core = info_ref[units + 2]
    triangle = lax.broadcasted_iota(jnp.int32, (UNIT, 2 * UNIT), 0) <= (
        lax.broadcasted_iota(jnp.int32, (UNIT, 2 * UNIT), 1) % UNIT
    )
    v_own = jnp.transpose(own_ref[:, HD:])

    def scores_of(unit, pair):
        return raw_scores(own_ref[: (unit + 1) * UNIT, :HD], head_pair((qm_ref, qo_ref), pair, unit))

    steps = [(unit, pair) for unit in range(units) for pair in range(4)]
    for (unit, pair), raw in ahead(steps, scores_of):
        low = info_ref[unit]
        blocks = []
        for b in range(unit + 1):
            block = raw[b * UNIT : (b + 1) * UNIT] + block_bias((low <= b) & (core == 0))
            blocks.append(jnp.where(triangle, block, NEG) if b == unit else block)
        scores = jnp.concatenate(blocks, axis=0)
        top = jnp.max(scores, axis=0, keepdims=True)
        weights = jnp.exp2((scores - top) * EXP_SCALE)
        total = jnp.sum(weights, axis=0, keepdims=True)
        store_state(out_ref, pair, unit, top, total, weighted(v_own[:, : (unit + 1) * UNIT], weights))


def attend_piece(which, info_ref, qm_ref, qo_ref, piece_ref, state_ref, out_ref, message_ref=None):
    units = qm_ref.shape[0] // UNIT
    v_piece = jnp.transpose(piece_ref[:, HD:])

    def scores_of(unit, pair):
        return raw_scores(piece_ref[:, :HD], head_pair((qm_ref, qo_ref), pair, unit))

    steps = [(unit, pair) for unit in range(units) for pair in range(4)]
    for (unit, pair), raw in ahead(steps, scores_of):
        bias = piece_bias(info_ref, unit, info_ref[units + which], units)
        scores = jnp.concatenate([raw[b * UNIT : (b + 1) * UNIT] + bias[b] for b in range(units)], axis=0)
        old_top, old_total, old_accum = load_state(state_ref, pair, unit)
        top = jnp.maximum(old_top, jnp.max(scores, axis=0, keepdims=True))
        weights = jnp.exp2((scores - top) * EXP_SCALE)
        factor = jnp.exp2((old_top - top) * EXP_SCALE)
        total = old_total * factor + jnp.sum(weights, axis=0, keepdims=True)
        accum = old_accum * factor + weighted(v_piece, weights)
        store_state(out_ref, pair, unit, top, total, accum)
        if message_ref is not None:
            for side in range(2):
                at = pl.ds((2 * pair + side) * HD, HD), pl.ds(unit * UNIT, UNIT)
                message_ref[at] = accum[:, side * UNIT : (side + 1) * UNIT].astype(jnp.bfloat16)
    if message_ref is not None:
        rest = out_ref[STATS:, :]
        for term in range(3):
            rounded = rest.astype(jnp.bfloat16)
            message_ref[pl.ds(STATS + 16 * term, 16), :] = rounded
            rest = rest - rounded.astype(jnp.float32)


def fetch(columns_ref, block, w_refs, w_buf, sems):
    depth, wide = w_buf.shape[1] // 2, w_buf.shape[2]
    at = pl.ds(pl.multiple_of(columns_ref[block] * wide, wide), wide)
    return [
        pltpu.make_async_copy(ref.at[:, at], w_buf.at[block, pl.ds(n * depth, depth)], sems.at[block, n])
        for n, ref in enumerate(w_refs)
    ]


def product(att_ref, w_buf, block):
    return jnp.dot(att_ref[...], w_buf[block], preferred_element_type=jnp.float32).astype(jnp.bfloat16)


def combine(columns_ref, here_ref, there_ref, wm_ref, wo_ref, att_ref, out_ref, w_buf, sems):
    heads = 8
    copies = fetch(columns_ref, 0, (wm_ref, wo_ref), w_buf, sems)
    for copy in copies:
        copy.start()
    here = here_ref[STATS:, :]
    there = sum(there_ref[pl.ds(STATS + 16 * term, 16), :].astype(jnp.float32) for term in (2, 1, 0))
    for head in range(heads):
        other = (head + heads // 2) % heads
        top_a, top_b = here[head : head + 1], there[other : other + 1]
        top = jnp.maximum(top_a, top_b)
        share_a = jnp.exp2((top_a - top) * EXP_SCALE)
        share_b = jnp.exp2((top_b - top) * EXP_SCALE)
        total = here[heads + head : heads + head + 1] * share_a + there[heads + other : heads + other + 1] * share_b
        accum = here_ref[pl.ds(head * HD, HD), :] * share_a
        accum += there_ref[pl.ds(other * HD, HD), :].astype(jnp.float32) * share_b
        att_ref[:, head * HD : (head + 1) * HD] = jnp.transpose(accum / total).astype(jnp.bfloat16)
    for copy in copies:
        copy.wait()
    out_ref[...] = product(att_ref, w_buf, 0)


def project(count, columns_ref, att_ref, wm_ref, wo_ref, *rest):
    out_refs, (w_buf, sems) = rest[:count], rest[count:]
    copies = [fetch(columns_ref, block, (wm_ref, wo_ref), w_buf, sems) for block in range(count)]
    for copy in sum(copies, []):
        copy.start()
    for block in range(count):
        for copy in copies[block]:
            copy.wait()
        out_refs[block][...] = product(att_ref, w_buf, block)


VM = pl.BlockSpec(memory_space=pltpu.VMEM)
HBM = pl.BlockSpec(memory_space=pltpu.HBM)
SM = pl.BlockSpec(memory_space=pltpu.SMEM)
LIMIT = pltpu.CompilerParams(vmem_limit_bytes=32 * 1024 * 1024)
WIDE_LIMIT = pltpu.CompilerParams(vmem_limit_bytes=49 * 1024 * 1024)


def on_device(lengths, queries, keys, values, out_weight):
    rows, wide = queries.shape
    units = rows // UNIT
    dp_count, y_count = lax.axis_size("dp"), lax.axis_size("y")
    dp, y, core = lax.axis_index("dp"), lax.axis_index("y"), lax.axis_index("core")
    swap = [(0, 1), (1, 0)]

    own = jnp.concatenate(
        [lax.dynamic_slice_in_dim(keys, y * HD, HD, 1), lax.dynamic_slice_in_dim(values, y * HD, HD, 1)], axis=1
    )
    first_pairs = [
        (2 * i + c, 2 * (i + FIRST_BACK[c]) + c) for c in range(2) for i in range(dp_count - FIRST_BACK[c])
    ]
    first = lax.ppermute(own, ("dp", "core"), first_pairs)
    own, q_sent = lax.optimization_barrier((own, queries))
    q_other = lax.ppermute(q_sent, "core", swap)
    second = lax.ppermute(first, "dp", [(i, i + 1) for i in range(dp_count - 1)])

    w_other = lax.ppermute(out_weight, "core", swap)

    order = jnp.arange(lengths.shape[0], dtype=jnp.int32)
    ends = jnp.sum(jnp.where(order[None, :] <= order[:, None], lengths[None, :], 0), axis=1)
    q_starts = dp * rows + UNIT * jnp.arange(units, dtype=jnp.int32)
    doc_starts = jnp.max(jnp.where(ends[None, :] <= q_starts[:, None], ends[None, :], 0), axis=1)
    lows = doc_starts // UNIT - dp * units
    tail = jnp.stack([1 + 2 * core, 2 + 2 * core, core])
    info = jnp.concatenate([lows, tail]).astype(jnp.int32)

    state_shape = jax.ShapeDtypeStruct((2 * wide + 16, rows), jnp.float32)
    state = pl.pallas_call(
        attend_own,
        out_shape=[state_shape],
        in_specs=[SM, VM, VM, VM],
        out_specs=[VM],
        compiler_params=LIMIT,
        cost_estimate=pl.CostEstimate(flops=OWN_FLOPS, bytes_accessed=4_000_000, transcendentals=1_000_000),
    )(info, queries, q_other, own)
    message_shape = jax.ShapeDtypeStruct((2 * wide + 48, rows), jnp.bfloat16)
    for which, piece in enumerate((first, second)):
        state = pl.pallas_call(
            functools.partial(attend_piece, which),
            out_shape=[state_shape, message_shape][: which + 1],
            in_specs=[SM, VM, VM, VM, VM],
            out_specs=[VM, VM][: which + 1],
            compiler_params=LIMIT,
            cost_estimate=pl.CostEstimate(flops=PIECE_FLOPS[which], bytes_accessed=6_000_000, transcendentals=1_000_000),
        )(info, queries, q_other, piece, state[0])
    state, message = state
    there = lax.ppermute(message, "core", swap)
    half = y_count // 2
    way = 1 - 2 * core

    def columns_at(distance):
        chunk = jnp.mod(y + way * distance, y_count)
        return jnp.stack([2 * chunk + core, 2 * chunk + 1 - core]).astype(jnp.int32)

    def w_scratch(count):
        return [pltpu.VMEM((count, 2 * wide, wide), jnp.bfloat16), pltpu.SemaphoreType.DMA((count, 2))]

    attended, farthest = pl.pallas_call(
        combine,
        out_shape=[
            jax.ShapeDtypeStruct((rows, 2 * wide), jnp.bfloat16),
            jax.ShapeDtypeStruct((rows, wide), jnp.bfloat16),
        ],
        in_specs=[SM, VM, VM, HBM, HBM],
        out_specs=[VM, VM],
        scratch_shapes=w_scratch(1),
        compiler_params=WIDE_LIMIT,
        cost_estimate=pl.CostEstimate(flops=400_000_000, bytes_accessed=5_000_000, transcendentals=10_000),
    )(columns_at(half)[:1], state, there, out_weight, w_other)

    def part(columns):
        count = columns.shape[0]
        return pl.pallas_call(
            functools.partial(project, count),
            out_shape=[jax.ShapeDtypeStruct((rows, wide), jnp.bfloat16)] * count,
            in_specs=[SM, VM, HBM, HBM],
            out_specs=[VM] * count,
            scratch_shapes=w_scratch(count),
            compiler_params=WIDE_LIMIT,
            cost_estimate=pl.CostEstimate(flops=PROJECT_FLOPS, bytes_accessed=10_000_000, transcendentals=0),
        )(columns, attended, out_weight, w_other)

    straight = [(2 * i + c, 2 * ((i + 1 - 2 * c) % y_count) + c) for i in range(y_count) for c in range(2)]
    cross = [(2 * i + c, 2 * ((i + 1 - 2 * c) % y_count) + 1 - c) for i in range(y_count) for c in range(2)]
    axes = ("y", "core")

    def add(a, *others):
        total = a.astype(jnp.float32)
        for b in others:
            total = total + b.astype(jnp.float32)
        return total.astype(jnp.bfloat16)

    near = lax.ppermute(farthest, axes, straight)
    now = part(columns_at(half - 1))
    far = lax.ppermute(now[1], axes, straight)
    for distance in range(half - 1, 0, -1):
        send = add(now[0], near)
        near = lax.ppermute(send, axes, straight)
        if distance > 1:
            columns = columns_at(distance - 1)
            if distance == 2:
                columns = jnp.concatenate([columns, columns_at(0)[:1]])
            now, send = lax.optimization_barrier((part(columns), send))
            send = add(now[1], far)
            far = lax.ppermute(send, axes, straight if distance > 2 else cross)
            now, send = lax.optimization_barrier((now, send))
    return add(now[2], near, far)


def solution(mesh):
    dp_count, tensor_count = mesh.shape["dp"], mesh.shape["tensor"]
    split = Mesh(mesh.devices.reshape(dp_count, tensor_count // 2, 2), ("dp", "y", "core"))
    heads = ("y", "core")
    placed = (P(), P("dp", heads), P("dp", None), P("dp", None), P(heads, None))
    return jax.shard_map(on_device, mesh=split, in_specs=placed, out_specs=P("dp", heads), check_vma=False)
```

```python
import functools
import math

import jax
import jax.numpy as jnp
from jax import lax
from jax.experimental import pallas as pl
from jax.experimental.pallas import tpu as pltpu
from jax.sharding import Mesh, PartitionSpec as P

HD = 128
UNIT = 128
NEG = -1e30
EXP_SCALE = math.log2(math.e) / HD**0.5
AHEAD = 3
OWN_FLOPS = 60_000_000_000
PIECE_FLOPS = (60_000_000_000, 60_000_000_000)
PROJECT_FLOPS = 60_000_000_000
STATS = 8 * HD

FIRST_BACK = (1, 3)
SECOND_BACK = (2, 4)


def block_bias(allowed):
    return jnp.where(allowed, 0.0, NEG).astype(jnp.float32)


def head_pair(q_refs, pair, unit):
    q_ref = q_refs[pair // 2]
    rows = pl.ds(unit * UNIT, UNIT)
    first = (pair % 2) * 2 * HD
    return jnp.concatenate([q_ref[rows, first : first + HD], q_ref[rows, first + HD : first + 2 * HD]], axis=0)


def raw_scores(k_rows, q_pair):
    return lax.dot_general(k_rows, q_pair, (((1,), (1,)), ((), ())), preferred_element_type=jnp.float32)


def weighted(v_columns, weights):
    return jnp.dot(v_columns, weights.astype(jnp.bfloat16), preferred_element_type=jnp.float32)


def ahead(steps, compute):
    pending = [compute(*step) for step in steps[:AHEAD]]
    for at, step in enumerate(steps):
        if at + AHEAD < len(steps):
            pending.append(compute(*steps[at + AHEAD]))
        yield step, pending.pop(0)


def store_state(out_ref, pair, unit, top, total, accum):
    heads = 8
    cols = pl.ds(unit * UNIT, UNIT)
    for side in range(2):
        head = 2 * pair + side
        part = slice(side * UNIT, (side + 1) * UNIT)
        out_ref[pl.ds(head * HD, HD), cols] = accum[:, part]
        out_ref[pl.ds(heads * HD + head, 1), cols] = top[:, part]
        out_ref[pl.ds(heads * HD + heads + head, 1), cols] = total[:, part]


def load_state(ref, pair, unit):
    heads = 8
    cols = pl.ds(unit * UNIT, UNIT)
    both = []
    for base, size in ((heads * HD, 1), (heads * HD + heads, 1), (0, HD)):
        halves = [ref[pl.ds(base + (2 * pair + side) * size, size), cols] for side in range(2)]
        both.append(jnp.concatenate(halves, axis=1))
    return both


def piece_bias(info_ref, unit, back, units):
    low = info_ref[unit]
    return [block_bias(low <= block - units * back) for block in range(units)]


def attend_own(info_ref, qm_ref, qo_ref, own_ref, out_ref):
    units = qm_ref.shape[0] // UNIT
    core = info_ref[units + 2]
    triangle = lax.broadcasted_iota(jnp.int32, (UNIT, 2 * UNIT), 0) <= (
        lax.broadcasted_iota(jnp.int32, (UNIT, 2 * UNIT), 1) % UNIT
    )
    v_own = jnp.transpose(own_ref[:, HD:])

    def scores_of(unit, pair):
        return raw_scores(own_ref[: (unit + 1) * UNIT, :HD], head_pair((qm_ref, qo_ref), pair, unit))

    steps = [(unit, pair) for unit in range(units) for pair in range(4)]
    for (unit, pair), raw in ahead(steps, scores_of):
        low = info_ref[unit]
        blocks = []
        for b in range(unit + 1):
            block = raw[b * UNIT : (b + 1) * UNIT] + block_bias((low <= b) & (core == 0))
            blocks.append(jnp.where(triangle, block, NEG) if b == unit else block)
        scores = jnp.concatenate(blocks, axis=0)
        top = jnp.max(scores, axis=0, keepdims=True)
        weights = jnp.exp2((scores - top) * EXP_SCALE)
        total = jnp.sum(weights, axis=0, keepdims=True)
        store_state(out_ref, pair, unit, top, total, weighted(v_own[:, : (unit + 1) * UNIT], weights))


def attend_piece(which, info_ref, qm_ref, qo_ref, piece_ref, state_ref, out_ref, message_ref=None):
    units = qm_ref.shape[0] // UNIT
    v_piece = jnp.transpose(piece_ref[:, HD:])

    def scores_of(unit, pair):
        return raw_scores(piece_ref[:, :HD], head_pair((qm_ref, qo_ref), pair, unit))

    steps = [(unit, pair) for unit in range(units) for pair in range(4)]
    for (unit, pair), raw in ahead(steps, scores_of):
        bias = piece_bias(info_ref, unit, info_ref[units + which], units)
        scores = jnp.concatenate([raw[b * UNIT : (b + 1) * UNIT] + bias[b] for b in range(units)], axis=0)
        old_top, old_total, old_accum = load_state(state_ref, pair, unit)
        top = jnp.maximum(old_top, jnp.max(scores, axis=0, keepdims=True))
        weights = jnp.exp2((scores - top) * EXP_SCALE)
        factor = jnp.exp2((old_top - top) * EXP_SCALE)
        total = old_total * factor + jnp.sum(weights, axis=0, keepdims=True)
        accum = old_accum * factor + weighted(v_piece, weights)
        store_state(out_ref, pair, unit, top, total, accum)
        if message_ref is not None:
            for side in range(2):
                at = pl.ds((2 * pair + side) * HD, HD), pl.ds(unit * UNIT, UNIT)
                message_ref[at] = accum[:, side * UNIT : (side + 1) * UNIT].astype(jnp.bfloat16)
    if message_ref is not None:
        rest = out_ref[STATS:, :]
        for term in range(3):
            rounded = rest.astype(jnp.bfloat16)
            message_ref[pl.ds(STATS + 16 * term, 16), :] = rounded
            rest = rest - rounded.astype(jnp.float32)


def fetch(columns_ref, block, w_refs, w_buf, sems):
    depth, wide = w_buf.shape[1] // 2, w_buf.shape[2]
    at = pl.ds(pl.multiple_of(columns_ref[block] * wide, wide), wide)
    return [
        pltpu.make_async_copy(ref.at[:, at], w_buf.at[block, pl.ds(n * depth, depth)], sems.at[block, n])
        for n, ref in enumerate(w_refs)
    ]


def product(att_ref, w_buf, block):
    return jnp.dot(att_ref[...], w_buf[block], preferred_element_type=jnp.float32).astype(jnp.bfloat16)


def combine(columns_ref, here_ref, there_ref, wm_ref, wo_ref, att_ref, *rest):
    heads = 8
    out_refs, (w_buf, sems) = rest[:-2], rest[-2:]
    copies = [fetch(columns_ref, block, (wm_ref, wo_ref), w_buf, sems) for block in range(len(out_refs))]
    for copy in sum(copies, []):
        copy.start()
    here = here_ref[STATS:, :]
    there = sum(there_ref[pl.ds(STATS + 16 * term, 16), :].astype(jnp.float32) for term in (2, 1, 0))
    for head in range(heads):
        other = (head + heads // 2) % heads
        top_a, top_b = here[head : head + 1], there[other : other + 1]
        top = jnp.maximum(top_a, top_b)
        share_a = jnp.exp2((top_a - top) * EXP_SCALE)
        share_b = jnp.exp2((top_b - top) * EXP_SCALE)
        total = here[heads + head : heads + head + 1] * share_a + there[heads + other : heads + other + 1] * share_b
        accum = here_ref[pl.ds(head * HD, HD), :] * share_a
        accum += there_ref[pl.ds(other * HD, HD), :].astype(jnp.float32) * share_b
        att_ref[:, head * HD : (head + 1) * HD] = jnp.transpose(accum / total).astype(jnp.bfloat16)
    for block, out_ref in enumerate(out_refs):
        for copy in copies[block]:
            copy.wait()
        out_ref[...] = product(att_ref, w_buf, block)


def project(count, columns_ref, att_ref, wm_ref, wo_ref, *rest):
    out_refs, (w_buf, sems) = rest[:count], rest[count:]
    copies = [fetch(columns_ref, block, (wm_ref, wo_ref), w_buf, sems) for block in range(count)]
    for copy in sum(copies, []):
        copy.start()
    for block in range(count):
        for copy in copies[block]:
            copy.wait()
        out_refs[block][...] = product(att_ref, w_buf, block)


VM = pl.BlockSpec(memory_space=pltpu.VMEM)
HBM = pl.BlockSpec(memory_space=pltpu.HBM)
SM = pl.BlockSpec(memory_space=pltpu.SMEM)
LIMIT = pltpu.CompilerParams(vmem_limit_bytes=32 * 1024 * 1024)
WIDE_LIMIT = pltpu.CompilerParams(vmem_limit_bytes=49 * 1024 * 1024)


def on_device(lengths, queries, keys, values, out_weight):
    rows, wide = queries.shape
    units = rows // UNIT
    dp_count, y_count = lax.axis_size("dp"), lax.axis_size("y")
    dp, y, core = lax.axis_index("dp"), lax.axis_index("y"), lax.axis_index("core")
    swap = [(0, 1), (1, 0)]

    own = jnp.concatenate(
        [lax.dynamic_slice_in_dim(keys, y * HD, HD, 1), lax.dynamic_slice_in_dim(values, y * HD, HD, 1)], axis=1
    )
    first_pairs = [
        (2 * i + c, 2 * (i + FIRST_BACK[c]) + c) for c in range(2) for i in range(dp_count - FIRST_BACK[c])
    ]
    first = lax.ppermute(own, ("dp", "core"), first_pairs)
    own, q_sent = lax.optimization_barrier((own, queries))
    q_other = lax.ppermute(q_sent, "core", swap)
    second = lax.ppermute(first, "dp", [(i, i + 1) for i in range(dp_count - 1)])

    w_other = lax.ppermute(out_weight, "core", swap)

    order = jnp.arange(lengths.shape[0], dtype=jnp.int32)
    ends = jnp.sum(jnp.where(order[None, :] <= order[:, None], lengths[None, :], 0), axis=1)
    q_starts = dp * rows + UNIT * jnp.arange(units, dtype=jnp.int32)
    doc_starts = jnp.max(jnp.where(ends[None, :] <= q_starts[:, None], ends[None, :], 0), axis=1)
    lows = doc_starts // UNIT - dp * units
    tail = jnp.stack([1 + 2 * core, 2 + 2 * core, core])
    info = jnp.concatenate([lows, tail]).astype(jnp.int32)

    state_shape = jax.ShapeDtypeStruct((2 * wide + 16, rows), jnp.float32)
    state = pl.pallas_call(
        attend_own,
        out_shape=[state_shape],
        in_specs=[SM, VM, VM, VM],
        out_specs=[VM],
        compiler_params=LIMIT,
        cost_estimate=pl.CostEstimate(flops=OWN_FLOPS, bytes_accessed=4_000_000, transcendentals=1_000_000),
    )(info, queries, q_other, own)
    message_shape = jax.ShapeDtypeStruct((2 * wide + 48, rows), jnp.bfloat16)
    for which, piece in enumerate((first, second)):
        state = pl.pallas_call(
            functools.partial(attend_piece, which),
            out_shape=[state_shape, message_shape][: which + 1],
            in_specs=[SM, VM, VM, VM, VM],
            out_specs=[VM, VM][: which + 1],
            compiler_params=LIMIT,
            cost_estimate=pl.CostEstimate(flops=PIECE_FLOPS[which], bytes_accessed=6_000_000, transcendentals=1_000_000),
        )(info, queries, q_other, piece, state[0])
    state, message = state
    there = lax.ppermute(message, "core", swap)
    half = y_count // 2
    way = 1 - 2 * core

    def columns_at(distance):
        chunk = jnp.mod(y + way * distance, y_count)
        return jnp.stack([2 * chunk + core, 2 * chunk + 1 - core]).astype(jnp.int32)

    def w_scratch(count):
        return [pltpu.VMEM((count, 2 * wide, wide), jnp.bfloat16), pltpu.SemaphoreType.DMA((count, 2))]

    attended, farthest, near, far = pl.pallas_call(
        combine,
        out_shape=[
            jax.ShapeDtypeStruct((rows, 2 * wide), jnp.bfloat16),
            *[jax.ShapeDtypeStruct((rows, wide), jnp.bfloat16)] * 3,
        ],
        in_specs=[SM, VM, VM, HBM, HBM],
        out_specs=[VM] * 4,
        scratch_shapes=w_scratch(3),
        compiler_params=WIDE_LIMIT,
        cost_estimate=pl.CostEstimate(flops=400_000_000, bytes_accessed=5_000_000, transcendentals=10_000),
    )(jnp.concatenate([columns_at(half)[:1], columns_at(half - 1)]), state, there, out_weight, w_other)

    def part(columns):
        count = columns.shape[0]
        return pl.pallas_call(
            functools.partial(project, count),
            out_shape=[jax.ShapeDtypeStruct((rows, wide), jnp.bfloat16)] * count,
            in_specs=[SM, VM, HBM, HBM],
            out_specs=[VM] * count,
            scratch_shapes=w_scratch(count),
            compiler_params=WIDE_LIMIT,
            cost_estimate=pl.CostEstimate(flops=PROJECT_FLOPS, bytes_accessed=10_000_000, transcendentals=0),
        )(columns, attended, out_weight, w_other)

    def carried(hops, crossing):
        return [
            (2 * i + c, 2 * ((i + (1 - 2 * c) * hops) % y_count) + (1 - c if crossing else c))
            for i in range(y_count)
            for c in range(2)
        ]

    straight = carried(1, False)
    axes = ("y", "core")

    def add(a, *others):
        total = a.astype(jnp.float32)
        for b in others:
            total = total + b.astype(jnp.float32)
        return total.astype(jnp.bfloat16)

    near = lax.ppermute(near, axes, straight)
    joining = [lax.ppermute(farthest, axes, carried(2, False))]
    far = lax.ppermute(far, axes, straight)
    rest = part(jnp.concatenate([*(columns_at(distance) for distance in range(half - 2, 0, -1)), columns_at(0)[:1]]))
    for distance in range(half - 2, 0, -1):
        send = add(rest[0], near, *joining)
        joining = []
        near = lax.ppermute(send, axes, straight)
        rest, send = lax.optimization_barrier((rest, send))
        send = add(rest[1], far)
        far = lax.ppermute(send, axes, straight if distance > 1 else carried(1, True))
        rest, send = lax.optimization_barrier((rest[2:], send))
    return add(rest[0], near, far)


def solution(mesh):
    dp_count, tensor_count = mesh.shape["dp"], mesh.shape["tensor"]
    split = Mesh(mesh.devices.reshape(dp_count, tensor_count // 2, 2), ("dp", "y", "core"))
    heads = ("y", "core")
    placed = (P(), P("dp", heads), P("dp", None), P("dp", None), P(heads, None))
    return jax.shard_map(on_device, mesh=split, in_specs=placed, out_specs=P("dp", heads), check_vma=False)
```

```python
import functools
import math

import jax
import jax.numpy as jnp
from jax import lax
from jax.experimental import pallas as pl
from jax.experimental.pallas import tpu as pltpu
from jax.sharding import Mesh, PartitionSpec as P

HD = 128
UNIT = 128
NEG = -1e30
EXP_SCALE = math.log2(math.e) / HD**0.5
AHEAD = 3
OWN_FLOPS = 60_000_000_000
PIECE_FLOPS = (60_000_000_000, 60_000_000_000)
PROJECT_FLOPS = 60_000_000_000
STATS = 8 * HD

FIRST_BACK = (1, 3)
SECOND_BACK = (2, 4)


def block_bias(allowed):
    return jnp.where(allowed, 0.0, NEG).astype(jnp.float32)


def head_pair(q_refs, pair, unit):
    q_ref = q_refs[pair // 2]
    rows = pl.ds(unit * UNIT, UNIT)
    first = (pair % 2) * 2 * HD
    return jnp.concatenate([q_ref[rows, first : first + HD], q_ref[rows, first + HD : first + 2 * HD]], axis=0)


def raw_scores(k_rows, q_pair):
    return lax.dot_general(k_rows, q_pair, (((1,), (1,)), ((), ())), preferred_element_type=jnp.float32)


def weighted(v_columns, weights):
    return jnp.dot(v_columns, weights.astype(jnp.bfloat16), preferred_element_type=jnp.float32)


def ahead(steps, compute):
    pending = [compute(*step) for step in steps[:AHEAD]]
    for at, step in enumerate(steps):
        if at + AHEAD < len(steps):
            pending.append(compute(*steps[at + AHEAD]))
        yield step, pending.pop(0)


def store_state(out_ref, pair, unit, top, total, accum):
    heads = 8
    cols = pl.ds(unit * UNIT, UNIT)
    for side in range(2):
        head = 2 * pair + side
        part = slice(side * UNIT, (side + 1) * UNIT)
        out_ref[pl.ds(head * HD, HD), cols] = accum[:, part]
        out_ref[pl.ds(heads * HD + head, 1), cols] = top[:, part]
        out_ref[pl.ds(heads * HD + heads + head, 1), cols] = total[:, part]


def load_state(ref, pair, unit):
    heads = 8
    cols = pl.ds(unit * UNIT, UNIT)
    both = []
    for base, size in ((heads * HD, 1), (heads * HD + heads, 1), (0, HD)):
        halves = [ref[pl.ds(base + (2 * pair + side) * size, size), cols] for side in range(2)]
        both.append(jnp.concatenate(halves, axis=1))
    return both


def piece_bias(info_ref, unit, back, units):
    low = info_ref[unit]
    return [block_bias(low <= block - units * back) for block in range(units)]


def attend_own(info_ref, qm_ref, qo_ref, own_ref, out_ref):
    units = qm_ref.shape[0] // UNIT
    core = info_ref[units + 2]
    triangle = lax.broadcasted_iota(jnp.int32, (UNIT, 2 * UNIT), 0) <= (
        lax.broadcasted_iota(jnp.int32, (UNIT, 2 * UNIT), 1) % UNIT
    )
    v_own = jnp.transpose(own_ref[:, HD:])

    def scores_of(unit, pair):
        return raw_scores(own_ref[: (unit + 1) * UNIT, :HD], head_pair((qm_ref, qo_ref), pair, unit))

    steps = [(unit, pair) for unit in range(units) for pair in range(4)]
    for (unit, pair), raw in ahead(steps, scores_of):
        low = info_ref[unit]
        blocks = []
        for b in range(unit + 1):
            block = raw[b * UNIT : (b + 1) * UNIT] + block_bias((low <= b) & (core == 0))
            blocks.append(jnp.where(triangle, block, NEG) if b == unit else block)
        scores = jnp.concatenate(blocks, axis=0)
        top = jnp.max(scores, axis=0, keepdims=True)
        weights = jnp.exp2((scores - top) * EXP_SCALE)
        total = jnp.sum(weights, axis=0, keepdims=True)
        store_state(out_ref, pair, unit, top, total, weighted(v_own[:, : (unit + 1) * UNIT], weights))


def attend_piece(which, info_ref, qm_ref, qo_ref, piece_ref, state_ref, out_ref, message_ref=None):
    units = qm_ref.shape[0] // UNIT
    v_piece = jnp.transpose(piece_ref[:, HD:])

    def scores_of(unit, pair):
        return raw_scores(piece_ref[:, :HD], head_pair((qm_ref, qo_ref), pair, unit))

    steps = [(unit, pair) for unit in range(units) for pair in range(4)]
    for (unit, pair), raw in ahead(steps, scores_of):
        bias = piece_bias(info_ref, unit, info_ref[units + which], units)
        scores = jnp.concatenate([raw[b * UNIT : (b + 1) * UNIT] + bias[b] for b in range(units)], axis=0)
        old_top, old_total, old_accum = load_state(state_ref, pair, unit)
        top = jnp.maximum(old_top, jnp.max(scores, axis=0, keepdims=True))
        weights = jnp.exp2((scores - top) * EXP_SCALE)
        factor = jnp.exp2((old_top - top) * EXP_SCALE)
        total = old_total * factor + jnp.sum(weights, axis=0, keepdims=True)
        accum = old_accum * factor + weighted(v_piece, weights)
        if message_ref is None:
            store_state(out_ref, pair, unit, top, total, accum)
        else:
            for side in range(2):
                at = pl.ds((2 * pair + side) * HD, HD), pl.ds(unit * UNIT, UNIT)
                part = slice(side * UNIT, (side + 1) * UNIT)
                message_ref[at] = accum[:, part].astype(jnp.bfloat16)
                out_ref[pl.ds(2 * pair + side, 1), at[1]] = top[:, part]
                out_ref[pl.ds(8 + 2 * pair + side, 1), at[1]] = total[:, part]
    if message_ref is not None:
        rest = out_ref[...]
        for term in range(3):
            rounded = rest.astype(jnp.bfloat16)
            message_ref[pl.ds(STATS + 16 * term, 16), :] = rounded
            rest = rest - rounded.astype(jnp.float32)


def fetch(columns_ref, block, w_refs, w_buf, sems):
    depth, wide = w_buf.shape[1] // 2, w_buf.shape[2]
    at = pl.ds(pl.multiple_of(columns_ref[block] * wide, wide), wide)
    return [
        pltpu.make_async_copy(ref.at[:, at], w_buf.at[block, pl.ds(n * depth, depth)], sems.at[block, n])
        for n, ref in enumerate(w_refs)
    ]


def product(att_ref, w_buf, block):
    return jnp.dot(att_ref[...], w_buf[block], preferred_element_type=jnp.float32).astype(jnp.bfloat16)


def combine(columns_ref, stats_ref, here_ref, there_ref, wm_ref, wo_ref, att_ref, out_ref, w_buf, sems):
    heads = 8
    copies = fetch(columns_ref, 0, (wm_ref, wo_ref), w_buf, sems)
    for copy in copies:
        copy.start()
    here = stats_ref[...]
    there = sum(there_ref[pl.ds(STATS + 16 * term, 16), :].astype(jnp.float32) for term in (2, 1, 0))
    for head in range(heads):
        other = (head + heads // 2) % heads
        top_a, top_b = here[head : head + 1], there[other : other + 1]
        top = jnp.maximum(top_a, top_b)
        share_a = jnp.exp2((top_a - top) * EXP_SCALE)
        share_b = jnp.exp2((top_b - top) * EXP_SCALE)
        total = here[heads + head : heads + head + 1] * share_a + there[heads + other : heads + other + 1] * share_b
        accum = here_ref[pl.ds(head * HD, HD), :].astype(jnp.float32) * share_a
        accum += there_ref[pl.ds(other * HD, HD), :].astype(jnp.float32) * share_b
        att_ref[:, head * HD : (head + 1) * HD] = jnp.transpose(accum / total).astype(jnp.bfloat16)
    for copy in copies:
        copy.wait()
    out_ref[...] = product(att_ref, w_buf, 0)


def project(count, columns_ref, att_ref, wm_ref, wo_ref, *rest):
    out_refs, (w_buf, sems) = rest[:count], rest[count:]
    copies = [fetch(columns_ref, block, (wm_ref, wo_ref), w_buf, sems) for block in range(count)]
    for copy in sum(copies, []):
        copy.start()
    for block in range(count):
        for copy in copies[block]:
            copy.wait()
        out_refs[block][...] = product(att_ref, w_buf, block)


VM = pl.BlockSpec(memory_space=pltpu.VMEM)
HBM = pl.BlockSpec(memory_space=pltpu.HBM)
SM = pl.BlockSpec(memory_space=pltpu.SMEM)
LIMIT = pltpu.CompilerParams(vmem_limit_bytes=32 * 1024 * 1024)
WIDE_LIMIT = pltpu.CompilerParams(vmem_limit_bytes=49 * 1024 * 1024)


def on_device(lengths, queries, keys, values, out_weight):
    rows, wide = queries.shape
    units = rows // UNIT
    dp_count, y_count = lax.axis_size("dp"), lax.axis_size("y")
    dp, y, core = lax.axis_index("dp"), lax.axis_index("y"), lax.axis_index("core")
    swap = [(0, 1), (1, 0)]

    own = jnp.concatenate(
        [lax.dynamic_slice_in_dim(keys, y * HD, HD, 1), lax.dynamic_slice_in_dim(values, y * HD, HD, 1)], axis=1
    )
    first_pairs = [
        (2 * i + c, 2 * (i + FIRST_BACK[c]) + c) for c in range(2) for i in range(dp_count - FIRST_BACK[c])
    ]
    first = lax.ppermute(own, ("dp", "core"), first_pairs)
    own, q_sent = lax.optimization_barrier((own, queries))
    q_other = lax.ppermute(q_sent, "core", swap)
    second = lax.ppermute(first, "dp", [(i, i + 1) for i in range(dp_count - 1)])

    w_other = lax.ppermute(out_weight, "core", swap)

    order = jnp.arange(lengths.shape[0], dtype=jnp.int32)
    ends = jnp.sum(jnp.where(order[None, :] <= order[:, None], lengths[None, :], 0), axis=1)
    q_starts = dp * rows + UNIT * jnp.arange(units, dtype=jnp.int32)
    doc_starts = jnp.max(jnp.where(ends[None, :] <= q_starts[:, None], ends[None, :], 0), axis=1)
    lows = doc_starts // UNIT - dp * units
    tail = jnp.stack([1 + 2 * core, 2 + 2 * core, core])
    info = jnp.concatenate([lows, tail]).astype(jnp.int32)

    state_shape = jax.ShapeDtypeStruct((2 * wide + 16, rows), jnp.float32)
    state = pl.pallas_call(
        attend_own,
        out_shape=[state_shape],
        in_specs=[SM, VM, VM, VM],
        out_specs=[VM],
        compiler_params=LIMIT,
        cost_estimate=pl.CostEstimate(flops=OWN_FLOPS, bytes_accessed=4_000_000, transcendentals=1_000_000),
    )(info, queries, q_other, own)
    stats_shape = jax.ShapeDtypeStruct((16, rows), jnp.float32)
    message_shape = jax.ShapeDtypeStruct((2 * wide + 48, rows), jnp.bfloat16)
    for which, piece in enumerate((first, second)):
        state = pl.pallas_call(
            functools.partial(attend_piece, which),
            out_shape=[state_shape] if which == 0 else [stats_shape, message_shape],
            in_specs=[SM, VM, VM, VM, VM],
            out_specs=[VM, VM][: which + 1],
            compiler_params=LIMIT,
            cost_estimate=pl.CostEstimate(flops=PIECE_FLOPS[which], bytes_accessed=6_000_000, transcendentals=1_000_000),
        )(info, queries, q_other, piece, state[0])
    stats, message = state
    there = lax.ppermute(message, "core", swap)
    half = y_count // 2
    way = 1 - 2 * core

    def columns_at(distance):
        chunk = jnp.mod(y + way * distance, y_count)
        return jnp.stack([2 * chunk + core, 2 * chunk + 1 - core]).astype(jnp.int32)

    def w_scratch(count):
        return [pltpu.VMEM((count, 2 * wide, wide), jnp.bfloat16), pltpu.SemaphoreType.DMA((count, 2))]

    attended, farthest = pl.pallas_call(
        combine,
        out_shape=[
            jax.ShapeDtypeStruct((rows, 2 * wide), jnp.bfloat16),
            jax.ShapeDtypeStruct((rows, wide), jnp.bfloat16),
        ],
        in_specs=[SM, VM, VM, VM, HBM, HBM],
        out_specs=[VM, VM],
        scratch_shapes=w_scratch(1),
        compiler_params=WIDE_LIMIT,
        cost_estimate=pl.CostEstimate(flops=400_000_000, bytes_accessed=5_000_000, transcendentals=10_000),
    )(columns_at(half)[:1], stats, message, there, out_weight, w_other)

    def part(columns):
        count = columns.shape[0]
        return pl.pallas_call(
            functools.partial(project, count),
            out_shape=[jax.ShapeDtypeStruct((rows, wide), jnp.bfloat16)] * count,
            in_specs=[SM, VM, HBM, HBM],
            out_specs=[VM] * count,
            scratch_shapes=w_scratch(count),
            compiler_params=WIDE_LIMIT,
            cost_estimate=pl.CostEstimate(flops=PROJECT_FLOPS, bytes_accessed=10_000_000, transcendentals=0),
        )(columns, attended, out_weight, w_other)

    straight = [(2 * i + c, 2 * ((i + 1 - 2 * c) % y_count) + c) for i in range(y_count) for c in range(2)]
    cross = [(2 * i + c, 2 * ((i + 1 - 2 * c) % y_count) + 1 - c) for i in range(y_count) for c in range(2)]
    axes = ("y", "core")

    def add(a, *others):
        total = a.astype(jnp.float32)
        for b in others:
            total = total + b.astype(jnp.float32)
        return total.astype(jnp.bfloat16)

    near = lax.ppermute(farthest, axes, straight)
    now = part(columns_at(half - 1))
    far = lax.ppermute(now[1], axes, straight)
    for distance in range(half - 1, 0, -1):
        send = add(now[0], near)
        near = lax.ppermute(send, axes, straight)
        if distance > 1:
            columns = columns_at(distance - 1)
            if distance == 2:
                columns = jnp.concatenate([columns, columns_at(0)[:1]])
            now, send = lax.optimization_barrier((part(columns), send))
            send = add(now[1], far)
            far = lax.ppermute(send, axes, straight if distance > 2 else cross)
            now, send = lax.optimization_barrier((now, send))
    return add(now[2], near, far)


def solution(mesh):
    dp_count, tensor_count = mesh.shape["dp"], mesh.shape["tensor"]
    split = Mesh(mesh.devices.reshape(dp_count, tensor_count // 2, 2), ("dp", "y", "core"))
    heads = ("y", "core")
    placed = (P(), P("dp", heads), P("dp", None), P("dp", None), P(heads, None))
    return jax.shard_map(on_device, mesh=split, in_specs=placed, out_specs=P("dp", heads), check_vma=False)
```
